512 devices in a mesh: ctx: 64 (over z_lo, x, core), head: 8 (over z_hi, y).
Axes of the slice: x: 4, y: 4, z: 16 (z_hi: 2, z_lo: 8; z = z_hi * 8 + z_lo), core: 2. Of those that a mesh axis runs over, the one named last changes fastest.
Arguments:
- queries: bfloat16 [24576, 7168], P('ctx', 'head'), may hold values from -160 to 160
- keys: bfloat16 [24576, 1024], P('ctx', 'head'), may hold values from -6 to 6
- values: bfloat16 [24576, 1024], P('ctx', 'head'), may hold values from -6 to 6
- out_grad: bfloat16 [24576, 7168], P('ctx', 'head'), may hold values from -6 to 6
- outputs: bfloat16 [24576, 7168], P('ctx', 'head'), may hold values from -4 to 4
- block_ids: int32 [128], replicated, may hold values from 0 to 127, each once
Outputs:
- grad_queries: bfloat16 [24576, 7168], P('ctx', 'head')
- grad_keys: bfloat16 [24576, 1024], P('ctx', 'head')
- grad_values: bfloat16 [24576, 1024], P('ctx', 'head')
- grad_square: float32 [], replicated
The draws below stay inside these ranges and needn't reach their ends.
All inputs are finite; a program needn't handle non-finite values.
Results may differ from the reference program's by a relative error of at most 0.015.
Values may be sent and summed in bfloat16 or wider, within the bound.
A program may use at most 64 MiB of HBM per device.

```python
import jax
import jax.numpy as jnp
from jax import lax

HD = 128
GROUP = 7
TOK_DEV = 384
BLK = 192
TOKENS = 24576
KV_HEADS = 8
QHEADS = 56
N_CTX = 64


def shared_keys(key):
    raw = jax.random.truncated_normal(jax.random.fold_in(key, 101), -6.0, 6.0, (TOKENS, KV_HEADS * HD), jnp.float32)
    return raw


def draw_keys(key, part):
    base = shared_keys(key)
    return base.astype(jnp.bfloat16)


def draw_queries(key, part):
    key = jax.random.fold_in(key, 7)
    raw = jax.random.truncated_normal(key, -6.0, 6.0, (TOKENS, QHEADS * HD), jnp.float32)
    return raw.astype(jnp.bfloat16)


def block_levels(own_key, extent, split, low, high):
    def one(dim, parts):
        steps = jax.random.uniform(jax.random.fold_in(jax.random.fold_in(own_key, 6), dim), (parts,), jnp.float32, low / len(split), high / len(split))
        return jnp.repeat(jnp.exp(steps), extent[dim] // parts).reshape((-1,) + (1,) * (len(extent) - dim - 1))

    level = one(*split[0])
    for cut in split[1:]:
        level = level * one(*cut)
    return level


def gaussian(rng, extent, width, limit, shards=(), held_as=jnp.bfloat16):
    result = jax.random.normal(rng, extent, jnp.float32) * width
    if len(shards) > 0:
        result = block_levels(rng, extent, shards, -0.22, 0.18) * result
    return jnp.clip(result, min=-limit, max=limit).astype(held_as)


def setup_inputs(seed: int = 0) -> dict:
    seeds = jax.random.split(jax.random.key(seed), 7)
    queries = draw_queries(jax.random.fold_in(seeds[6], 71), 0)
    keys = draw_keys(jax.random.fold_in(seeds[6], 71), 0)
    values = gaussian(seeds[2], (TOKENS, KV_HEADS * HD), 1.0, 6.0, ((0, 64), (1, 8)))
    out_grad = gaussian(seeds[3], (TOKENS, QHEADS * HD), 1.0, 6.0, ((0, 64), (1, 8)))
    outputs = gaussian(seeds[4], (TOKENS, QHEADS * HD), 0.5, 4.0, ((0, 64), (1, 8)))
    block_ids = jax.random.permutation(seeds[5], 2 * N_CTX).astype(jnp.int32)
    return {"queries": queries, "keys": keys, "values": values, "out_grad": out_grad, "outputs": outputs, "block_ids": block_ids}


NEG = -1.0e30


def rounded(x):
    return lax.optimization_barrier(x.astype(jnp.bfloat16)).astype(jnp.float32)


def reference(queries, keys, values, out_grad, outputs, block_ids):
    scale = HD ** -0.5
    rows = jnp.arange(TOK_DEV, dtype=jnp.int32)

    def pos_of(device):
        first = block_ids[2 * device]
        second = block_ids[2 * device + 1]
        return jnp.where(rows < BLK, first * BLK + rows, second * BLK + rows - BLK).astype(jnp.int32)

    qall = queries.reshape(N_CTX, TOK_DEV, KV_HEADS, GROUP, HD)
    kall = keys.reshape(N_CTX, TOK_DEV, KV_HEADS, HD)
    vall = values.reshape(N_CTX, TOK_DEV, KV_HEADS, HD)
    dall = out_grad.reshape(N_CTX, TOK_DEV, KV_HEADS, GROUP, HD)
    oall = outputs.reshape(N_CTX, TOK_DEV, KV_HEADS, GROUP, HD)

    def one(place):
        left = (place - 1) % N_CTX
        right = (place + 1) % N_CTX
        kf = jnp.concatenate([kall[left], kall[place], kall[right]], 0).astype(jnp.float32)
        vf = jnp.concatenate([vall[left], vall[place], vall[right]], 0).astype(jnp.float32)
        pos_k = jnp.concatenate([pos_of(left), pos_of(place), pos_of(right)], 0)
        pos_q = pos_of(place)
        qf = qall[place].astype(jnp.float32)
        dof = dall[place].astype(jnp.float32)
        of = oall[place].astype(jnp.float32)
        seen = (pos_k[None, :] <= pos_q[:, None])[None, None]
        scores = jnp.einsum("tgjd,ugd->gjtu", qf, kf) * scale
        scores = jnp.where(seen, scores, NEG)
        peak = jnp.max(scores, axis=-1)
        total = jnp.sum(jnp.where(seen, jnp.exp(scores - peak[..., None]), 0.0), axis=-1)
        lse = peak + jnp.log(total)
        probs = jnp.where(seen, jnp.exp(scores - lse[..., None]), 0.0)
        probs_low = rounded(probs)
        dprobs = jnp.einsum("tgjd,ugd->gjtu", dof, vf)
        delta = jnp.transpose(jnp.sum(dof * of, axis=-1), (1, 2, 0))
        dscore = rounded(probs * (dprobs - delta[..., None]) * scale)
        grad_v = jnp.einsum("gjtu,tgjd->ugd", probs_low, dof)
        grad_k = jnp.einsum("gjtu,tgjd->ugd", dscore, qf)
        grad_q = jnp.einsum("gjtu,ugd->tgjd", dscore, kf)
        return grad_q, grad_k.reshape(3, TOK_DEV, KV_HEADS, HD), grad_v.reshape(3, TOK_DEV, KV_HEADS, HD)

    grad_q, part_k, part_v = lax.map(one, jnp.arange(N_CTX, dtype=jnp.int32))
    grad_k = part_k[:, 1] + jnp.roll(part_k[:, 0], -1, axis=0) + jnp.roll(part_k[:, 2], 1, axis=0)
    grad_v = part_v[:, 1] + jnp.roll(part_v[:, 0], -1, axis=0) + jnp.roll(part_v[:, 2], 1, axis=0)
    count = TOKENS * (QHEADS + 2 * KV_HEADS) * HD
    grad_square = (jnp.sum(grad_q * grad_q) + jnp.sum(grad_k * grad_k) + jnp.sum(grad_v * grad_v)) / count
    grad_queries = grad_q.reshape(TOKENS, QHEADS * HD).astype(jnp.bfloat16)
    grad_keys = grad_k.reshape(TOKENS, KV_HEADS * HD).astype(jnp.bfloat16)
    grad_values = grad_v.reshape(TOKENS, KV_HEADS * HD).astype(jnp.bfloat16)
    return grad_queries, grad_keys, grad_values, grad_square
```

```python
import jax
import jax.numpy as jnp
from jax import lax
from jax.experimental import pallas as pl
from jax.experimental.pallas import tpu as pltpu
from jax.sharding import PartitionSpec as P

HD = 128
GROUP = 7
TOK = 384
BLK = 192
N_CTX = 64
SCALE = HD**-0.5
EXP2_SCALE = SCALE * 1.4426950408889634
NEG = -1e30
BIG = 1e30
HEAD_SETS = ((0, 1), (2, 3), (4, 5), (6,))
OWN, NEAR, FAR = 0, 1, 2
MESH = pl.DeviceIdType.MESH
f32 = jnp.float32
bf16 = jnp.bfloat16


def dot_nt(a, b):
    return lax.dot_general(a, b, (((1,), (1,)), ((), ())), preferred_element_type=f32)


def dot_nn(a, b):
    return lax.dot_general(a, b, (((1,), (0,)), ((), ())), preferred_element_type=f32)


def fold(x):
    rows, cols = x.shape
    y = jnp.sum(x.reshape(rows // 8, 8, cols), axis=0)
    out = y[:, :128]
    for c in range(128, cols, 128):
        out = out + y[:, c : c + 128]
    return out


def kernel(
    q_hbm, k_hbm, v_hbm, do_hbm, o_hbm, ids,
    gq_hbm, gk_hbm, gv_hbm, sq_out,
    q, do, o, kv, s, dpd, p, ds, delta, mask, acc, gq, gkv,
    part, back, red, red_src,
    load_sem, out_sem, kv_send, kv_recv, part_send, part_recv, red_send, red_recv,
):
    me = lax.axis_index("ctx")
    hd = lax.axis_index("head")
    core = lax.rem(me, 2)
    near = me + 1 - 2 * core
    far = lax.rem(me + N_CTX - 1 + 2 * core, N_CTX)
    plane = me // 8
    spot = lax.rem(me, 8)
    others = {NEAR: near, FAR: far}

    partners = [[], [], []]
    for j in range(1, 8):
        partners[0].append({"ctx": plane * 8 + lax.rem(spot + j, 8), "head": hd})
        partners[1].append({"ctx": me, "head": lax.rem(hd + j, 8)})
        partners[2].append({"ctx": lax.rem(plane + j, 8) * 8 + spot, "head": hd})

    loads = [
        pltpu.make_async_copy(src, dst, load_sem.at[i])
        for i, (src, dst) in enumerate(
            [(q_hbm, q), (k_hbm, kv.at[0, OWN]), (v_hbm, kv.at[1, OWN]), (do_hbm, do), (o_hbm, o)]
        )
    ]
    for c in loads:
        c.start()
    barrier = pltpu.get_barrier_semaphore()
    greet = [{"ctx": near, "head": hd}, {"ctx": far, "head": hd}] + sum(partners, [])
    for dev in greet:
        pl.semaphore_signal(barrier, inc=1, device_id=dev, device_id_type=MESH)
    pl.semaphore_wait(barrier, len(greet))

    sends = {}
    for i, src in ((0, k_hbm), (1, v_hbm)):
        for side in (FAR, NEAR):
            c = pltpu.make_async_remote_copy(
                src_ref=src,
                dst_ref=kv.at[i, side],
                send_sem=kv_send.at[i, side],
                recv_sem=kv_recv.at[i, side],
                device_id={"ctx": others[side], "head": hd},
                device_id_type=MESH,
            )
            c.start()
            sends[i, side] = c

    lane = lax.broadcasted_iota(jnp.int32, (1, TOK), 1)
    row = lax.broadcasted_iota(jnp.int32, (TOK, 1), 0)
    id0, id1 = ids[2 * me], ids[2 * me + 1]
    qid = jnp.where(lane < BLK, id0, id1)
    pos_q = qid * BLK + jnp.where(lane < BLK, lane, lane - BLK)
    pos_k = jnp.where(row < BLK, id0 * BLK + row, id1 * BLK + row - BLK)
    mask[...] = jnp.where(pos_k <= pos_q, 0.0, NEG).astype(f32)
    seen = {
        side: [jnp.where(ids[2 * others[side] + b] < qid, 1, 0) for b in (0, 1)]
        for side in (NEAR, FAR)
    }

    for c in loads:
        c.wait()

    cols = lax.broadcasted_iota(jnp.int32, (TOK, HD), 1)
    gather = jnp.zeros((TOK, HD), f32)
    for h in range(GROUP):
        c = slice(h * HD, (h + 1) * HD)
        d = jnp.sum(do[:, c].astype(f32) * o[:, c].astype(f32), axis=1, keepdims=True)
        gather = jnp.where(cols == h, d, gather)
    delta[...] = gather.T[:8]

    def stack(ref, hs):
        return jnp.concatenate([ref[:, h * HD : (h + 1) * HD] for h in hs], axis=0)

    def rep(x, n):
        return jnp.concatenate([x] * n, axis=1)

    def span(hs):
        return slice(hs[0] * TOK, (hs[-1] + 1) * TOK)

    def rows(side):
        return slice(side * TOK, (side + 1) * TOK)

    peaks = {}

    def scores(side, hs):
        x = dot_nt(kv[0, side], stack(q, hs))
        if side == OWN:
            x = x + rep(mask[...], len(hs))
            peaks[side, hs] = [jnp.max(x, axis=0, keepdims=True)]
        else:
            peaks[side, hs] = [
                jnp.max(x[b * BLK : (b + 1) * BLK], axis=0, keepdims=True) for b in (0, 1)
            ]
        s[rows(side), span(hs)] = x

    def dprobs(side, hs):
        row_delta = jnp.concatenate([delta[h : h + 1] for h in hs], axis=1)
        return (dot_nt(kv[1, side], stack(do, hs)) - row_delta).astype(bf16)

    for hs in HEAD_SETS:
        scores(OWN, hs)
        dpd[rows(OWN), span(hs)] = dprobs(OWN, hs)
    sends[0, NEAR].wait_recv()
    sends[1, NEAR].wait_recv()
    for hs in HEAD_SETS:
        scores(NEAR, hs)
        dpd[rows(NEAR), span(hs)] = dprobs(NEAR, hs)
    sends[0, FAR].wait_recv()
    sends[1, FAR].wait_recv()

    norm = {}
    scaled = {}

    def softmax(hs):
        n = len(hs)
        m = peaks[OWN, hs][0]
        vis = {}
        for side in (NEAR, FAR):
            for b in (0, 1):
                vis[side, b] = rep(seen[side][b], n) > 0
                m = jnp.maximum(m, jnp.where(vis[side, b], peaks[side, hs][b], NEG))
        e = jnp.exp2((s[rows(OWN), span(hs)] - m) * EXP2_SCALE)
        total = jnp.sum(e, axis=0, keepdims=True)
        p[rows(OWN), span(hs)] = e.astype(bf16)
        for side in (NEAR, FAR):
            for b in (0, 1):
                r = slice(side * TOK + b * BLK, side * TOK + (b + 1) * BLK)
                shift = jnp.where(vis[side, b], m, BIG)
                e = jnp.exp2((s[r, span(hs)] - shift) * EXP2_SCALE)
                total = total + jnp.sum(e, axis=0, keepdims=True)
                p[r, span(hs)] = e.astype(bf16)
        inv = 1.0 / total
        norm[hs] = inv * SCALE
        cols_inv = jnp.concatenate(
            [
                jnp.broadcast_to(inv[:, i * TOK : (i + 1) * TOK], (HD, TOK)).T
                for i in range(n)
            ],
            axis=0,
        )
        scaled[hs] = (
            (stack(q, hs).astype(f32) * (cols_inv * SCALE)).astype(bf16),
            (stack(do, hs).astype(f32) * cols_inv).astype(bf16),
        )

    def key_grads(side, hs, first):
        r, c = rows(side), span(hs)
        qn, don = scaled[hs]
        if side == FAR:
            d = dprobs(FAR, hs)
        else:
            d = dpd[r, c]
        w = p[r, c]
        dsv = d * w
        ds[r, c] = dsv
        gk = dot_nn(dsv, qn)
        gv = dot_nn(w, don)
        if first:
            acc[0, side], acc[1, side] = gk, gv
        else:
            acc[0, side] += gk
            acc[1, side] += gv

    def send_back(side):
        out = []
        for i in (0, 1):
            part[i, side - 1] = acc[i, side].astype(bf16)
            c = pltpu.make_async_remote_copy(
                src_ref=part.at[i, side - 1],
                dst_ref=back.at[i, side - 1],
                send_sem=part_send.at[i, side - 1],
                recv_sem=part_recv.at[i, side - 1],
                device_id={"ctx": others[side], "head": hd},
                device_id_type=MESH,
            )
            c.start()
            out.append(c)
        return out

    scores(FAR, HEAD_SETS[0])
    for n, hs in enumerate(HEAD_SETS):
        if n + 1 < len(HEAD_SETS):
            scores(FAR, HEAD_SETS[n + 1])
        softmax(hs)
        key_grads(FAR, hs, n == 0)
    returns = {FAR: send_back(FAR)}
    for n, hs in enumerate(HEAD_SETS):
        key_grads(NEAR, hs, n == 0)
    returns[NEAR] = send_back(NEAR)
    for n, hs in enumerate(HEAD_SETS):
        key_grads(OWN, hs, n == 0)

    square = jnp.zeros((8, 128), f32)
    k_t = kv[0].reshape(3 * TOK, HD).T
    for hs in HEAD_SETS:
        g = dot_nn(k_t, ds[:, span(hs)]) * norm[hs]
        square = square + fold(g * g)
        for i, h in enumerate(hs):
            gq[:, h * HD : (h + 1) * HD] = g[:, i * TOK : (i + 1) * TOK].T.astype(bf16)
    outs = [pltpu.make_async_copy(gq, gq_hbm, out_sem.at[0])]
    outs[0].start()

    for side in (NEAR, FAR):
        for c in returns[side]:
            c.wait_recv()
    for i, dst in ((0, gk_hbm), (1, gv_hbm)):
        g = acc[i, OWN] + back[i, 0].astype(f32) + back[i, 1].astype(f32)
        square = square + fold(g * g)
        gkv[i] = g.astype(bf16)
        c = pltpu.make_async_copy(gkv.at[i], dst, out_sem.at[1 + i])
        c.start()
        outs.append(c)

    sent = []
    for r, place in enumerate((spot, hd, plane)):
        red_src[r] = square
        red[r, place] = square
        copies = []
        for j in range(1, 8):
            c = pltpu.make_async_remote_copy(
                src_ref=red_src.at[r],
                dst_ref=red.at[r, place],
                send_sem=red_send.at[r, j],
                recv_sem=red_recv.at[r, j],
                device_id=partners[r][j - 1],
                device_id_type=MESH,
            )
            c.start()
            copies.append(c)
        for c in copies:
            c.wait_recv()
        sent += copies
        square = red[r, 0]
        for j in range(1, 8):
            square = square + red[r, j]
    count = TOK * N_CTX * 8 * (GROUP + 2) * HD
    sq_out[0, 0] = jnp.sum(square) / count

    for c in sent + list(sends.values()) + returns[NEAR] + returns[FAR]:
        c.wait_send()
    for c in outs:
        c.wait()


def shards(queries, keys, values, out_grad, outputs, block_ids):
    hbm = pl.BlockSpec(memory_space=pl.ANY)
    smem = pl.BlockSpec(memory_space=pltpu.SMEM)
    wide = GROUP * TOK
    dma = pltpu.SemaphoreType.DMA
    gq, gk, gv, square = pl.pallas_call(
        kernel,
        out_shape=(
            jax.ShapeDtypeStruct((TOK, GROUP * HD), bf16),
            jax.ShapeDtypeStruct((TOK, HD), bf16),
            jax.ShapeDtypeStruct((TOK, HD), bf16),
            jax.ShapeDtypeStruct((1, 1), f32),
        ),
        in_specs=[hbm] * 5 + [smem],
        out_specs=(hbm, hbm, hbm, smem),
        scratch_shapes=[
            pltpu.VMEM((TOK, GROUP * HD), bf16),
            pltpu.VMEM((TOK, GROUP * HD), bf16),
            pltpu.VMEM((TOK, GROUP * HD), bf16),
            pltpu.VMEM((2, 3, TOK, HD), bf16),
            pltpu.VMEM((3 * TOK, wide), f32),
            pltpu.VMEM((2 * TOK, wide), bf16),
            pltpu.VMEM((3 * TOK, wide), bf16),
            pltpu.VMEM((3 * TOK, wide), bf16),
            pltpu.VMEM((8, TOK), f32),
            pltpu.VMEM((TOK, TOK), f32),
            pltpu.VMEM((2, 3, TOK, HD), f32),
            pltpu.VMEM((TOK, GROUP * HD), bf16),
            pltpu.VMEM((2, TOK, HD), bf16),
            pltpu.VMEM((2, 2, TOK, HD), bf16),
            pltpu.VMEM((2, 2, TOK, HD), bf16),
            pltpu.VMEM((3, 8, 8, 128), f32),
            pltpu.VMEM((3, 8, 128), f32),
            dma((5,)),
            dma((3,)),
            dma((2, 3)),
            dma((2, 3)),
            dma((2, 2)),
            dma((2, 2)),
            dma((3, 8)),
            dma((3, 8)),
        ],
        compiler_params=pltpu.CompilerParams(
            collective_id=0, has_side_effects=True, vmem_limit_bytes=56 * 2**20
        ),
        name="grads",
    )(queries, keys, values, out_grad, outputs, block_ids)
    return gq, gk, gv, square.reshape(())


def solution(mesh):
    return jax.shard_map(
        shards,
        mesh=mesh,
        in_specs=(
            P("ctx", "head"),
            P("ctx", "head"),
            P("ctx", "head"),
            P("ctx", "head"),
            P("ctx", "head"),
            P(),
        ),
        out_specs=(P("ctx", "head"), P("ctx", "head"), P("ctx", "head"), P()),
        check_vma=False,
    )
```

```python
import jax
import jax.numpy as jnp
from jax import lax
from jax.experimental import pallas as pl
from jax.experimental.pallas import tpu as pltpu
from jax.sharding import PartitionSpec as P

HD = 128
GROUP = 7
TOK = 384
BLK = 192
N_CTX = 64
SCALE = HD**-0.5
EXP2_SCALE = SCALE * 1.4426950408889634
NEG = -1e30
BIG = 1e30
HEAD_SETS = ((0, 1), (2, 3), (4, 5), (6,))
OWN, NEAR, FAR = 0, 1, 2
MESH = pl.DeviceIdType.MESH
f32 = jnp.float32
bf16 = jnp.bfloat16


def dot_nt(a, b):
    return lax.dot_general(a, b, (((1,), (1,)), ((), ())), preferred_element_type=f32)


def dot_nn(a, b):
    return lax.dot_general(a, b, (((1,), (0,)), ((), ())), preferred_element_type=f32)


def fold(x):
    rows, cols = x.shape
    y = jnp.sum(x.reshape(rows // 8, 8, cols), axis=0)
    out = y[:, :128]
    for c in range(128, cols, 128):
        out = out + y[:, c : c + 128]
    return out


def kernel(
    q_hbm, k_hbm, v_hbm, do_hbm, o_hbm, ids,
    gq_hbm, gk_hbm, gv_hbm, sq_out,
    q, do, o, kv, s, dpd, p, ds, delta, mask, acc, gq, gkv,
    part, back, red_a, red_b, red_src,
    load_sem, out_sem, kv_send, kv_recv, part_send, part_recv, red_send, red_recv,
):
    me = lax.axis_index("ctx")
    hd = lax.axis_index("head")
    core = lax.rem(me, 2)
    near = me + 1 - 2 * core
    far = lax.rem(me + N_CTX - 1 + 2 * core, N_CTX)
    plane = me // 8
    spot = lax.rem(me, 8)
    others = {NEAR: near, FAR: far}

    y = lax.rem(hd, 4)
    deep = (hd // 4) * 8 + plane

    def across(j):
        return {"ctx": plane * 8 + lax.rem(spot + j % 8, 8), "head": hd - y + lax.rem(y + j // 8, 4)}

    def along(j):
        z = lax.rem(deep + j, 16)
        return {"ctx": lax.rem(z, 8) * 8 + spot, "head": (z // 8) * 4 + y}

    partners = [[across(j) for j in range(1, 32)], [along(j) for j in range(1, 16)]]

    barrier = pltpu.get_barrier_semaphore()
    greet = [{"ctx": far, "head": hd}, {"ctx": near, "head": hd}] + partners[0] + partners[1]
    for dev in greet:
        pl.semaphore_signal(barrier, inc=1, device_id=dev, device_id_type=MESH)
    loads = [
        pltpu.make_async_copy(src, dst, load_sem.at[i])
        for i, (src, dst) in enumerate(
            [(q_hbm, q), (k_hbm, kv.at[0, OWN]), (v_hbm, kv.at[1, OWN]), (do_hbm, do), (o_hbm, o)]
        )
    ]
    for c in loads:
        c.start()
    pl.semaphore_wait(barrier, len(greet))

    sends = {}
    for i, src in ((0, k_hbm), (1, v_hbm)):
        for side in (FAR, NEAR):
            c = pltpu.make_async_remote_copy(
                src_ref=src,
                dst_ref=kv.at[i, side],
                send_sem=kv_send.at[i, side],
                recv_sem=kv_recv.at[i, side],
                device_id={"ctx": others[side], "head": hd},
                device_id_type=MESH,
            )
            c.start()
            sends[i, side] = c

    lane = lax.broadcasted_iota(jnp.int32, (1, TOK), 1)
    row = lax.broadcasted_iota(jnp.int32, (TOK, 1), 0)
    id0, id1 = ids[2 * me], ids[2 * me + 1]
    qid = jnp.where(lane < BLK, id0, id1)
    pos_q = qid * BLK + jnp.where(lane < BLK, lane, lane - BLK)
    pos_k = jnp.where(row < BLK, id0 * BLK + row, id1 * BLK + row - BLK)
    mask[...] = jnp.where(pos_k <= pos_q, 0.0, NEG).astype(f32)
    seen = {
        side: [jnp.where(ids[2 * others[side] + b] < qid, 1, 0) for b in (0, 1)]
        for side in (NEAR, FAR)
    }

    for c in loads:
        c.wait()

    cols = lax.broadcasted_iota(jnp.int32, (TOK, HD), 1)
    gather = jnp.zeros((TOK, HD), f32)
    for h in range(GROUP):
        c = slice(h * HD, (h + 1) * HD)
        d = jnp.sum(do[:, c].astype(f32) * o[:, c].astype(f32), axis=1, keepdims=True)
        gather = jnp.where(cols == h, d, gather)
    delta[...] = gather.T[:8]

    def stack(ref, hs):
        return jnp.concatenate([ref[:, h * HD : (h + 1) * HD] for h in hs], axis=0)

    def rep(x, n):
        return jnp.concatenate([x] * n, axis=1)

    def span(hs):
        return slice(hs[0] * TOK, (hs[-1] + 1) * TOK)

    def rows(side):
        return slice(side * TOK, (side + 1) * TOK)

    peaks = {}

    def scores(side, hs):
        x = dot_nt(kv[0, side], stack(q, hs))
        if side == OWN:
            x = x + rep(mask[...], len(hs))
            peaks[side, hs] = [jnp.max(x, axis=0, keepdims=True)]
        else:
            peaks[side, hs] = [
                jnp.max(x[b * BLK : (b + 1) * BLK], axis=0, keepdims=True) for b in (0, 1)
            ]
        s[rows(side), span(hs)] = x

    def dprobs(side, hs):
        row_delta = jnp.concatenate([delta[h : h + 1] for h in hs], axis=1)
        return (dot_nt(kv[1, side], stack(do, hs)) - row_delta).astype(bf16)

    for hs in HEAD_SETS:
        scores(OWN, hs)
        dpd[rows(OWN), span(hs)] = dprobs(OWN, hs)
    sends[0, NEAR].wait_recv()
    sends[1, NEAR].wait_recv()
    for hs in HEAD_SETS:
        scores(NEAR, hs)
        dpd[rows(NEAR), span(hs)] = dprobs(NEAR, hs)
    sends[0, FAR].wait_recv()
    sends[1, FAR].wait_recv()

    norm = {}
    scaled = {}

    def softmax(hs):
        n = len(hs)
        m = peaks[OWN, hs][0]
        vis = {}
        for side in (NEAR, FAR):
            for b in (0, 1):
                vis[side, b] = rep(seen[side][b], n) > 0
                m = jnp.maximum(m, jnp.where(vis[side, b], peaks[side, hs][b], NEG))
        e = jnp.exp2((s[rows(OWN), span(hs)] - m) * EXP2_SCALE)
        total = jnp.sum(e, axis=0, keepdims=True)
        p[rows(OWN), span(hs)] = e.astype(bf16)
        for side in (NEAR, FAR):
            for b in (0, 1):
                r = slice(side * TOK + b * BLK, side * TOK + (b + 1) * BLK)
                shift = jnp.where(vis[side, b], m, BIG)
                e = jnp.exp2((s[r, span(hs)] - shift) * EXP2_SCALE)
                total = total + jnp.sum(e, axis=0, keepdims=True)
                p[r, span(hs)] = e.astype(bf16)
        inv = 1.0 / total
        norm[hs] = inv * SCALE
        cols_inv = jnp.concatenate(
            [
                jnp.broadcast_to(inv[:, i * TOK : (i + 1) * TOK], (HD, TOK)).T
                for i in range(n)
            ],
            axis=0,
        )
        scaled[hs] = (
            (stack(q, hs).astype(f32) * (cols_inv * SCALE)).astype(bf16),
            (stack(do, hs).astype(f32) * cols_inv).astype(bf16),
        )

    def key_grads(side, hs, first):
        r, c = rows(side), span(hs)
        qn, don = scaled[hs]
        if side == FAR:
            d = dprobs(FAR, hs)
        else:
            d = dpd[r, c]
        w = p[r, c]
        dsv = d * w
        ds[r, c] = dsv
        gk = dot_nn(dsv, qn)
        gv = dot_nn(w, don)
        if first:
            acc[0, side], acc[1, side] = gk, gv
        else:
            acc[0, side] += gk
            acc[1, side] += gv

    def send_back(side):
        out = []
        for i in (0, 1):
            part[i, side - 1] = acc[i, side].astype(bf16)
            c = pltpu.make_async_remote_copy(
                src_ref=part.at[i, side - 1],
                dst_ref=back.at[i, side - 1],
                send_sem=part_send.at[i, side - 1],
                recv_sem=part_recv.at[i, side - 1],
                device_id={"ctx": others[side], "head": hd},
                device_id_type=MESH,
            )
            c.start()
            out.append(c)
        return out

    scores(FAR, HEAD_SETS[0])
    for n, hs in enumerate(HEAD_SETS):
        if n + 1 < len(HEAD_SETS):
            scores(FAR, HEAD_SETS[n + 1])
        softmax(hs)
        key_grads(FAR, hs, n == 0)
    returns = {FAR: send_back(FAR)}
    for n, hs in enumerate(HEAD_SETS):
        key_grads(NEAR, hs, n == 0)
    returns[NEAR] = send_back(NEAR)
    for n, hs in enumerate(HEAD_SETS):
        key_grads(OWN, hs, n == 0)

    square = jnp.zeros((8, 128), f32)
    k_t = kv[0].reshape(3 * TOK, HD).T
    for hs in HEAD_SETS:
        g = dot_nn(k_t, ds[:, span(hs)]) * norm[hs]
        square = square + fold(g * g)
        for i, h in enumerate(hs):
            gq[:, h * HD : (h + 1) * HD] = g[:, i * TOK : (i + 1) * TOK].T.astype(bf16)

    outs = [pltpu.make_async_copy(gq, gq_hbm, out_sem.at[0])]
    outs[0].start()

    for side in (NEAR, FAR):
        for c in returns[side]:
            c.wait_recv()
    for i, dst in ((0, gk_hbm), (1, gv_hbm)):
        g = acc[i, OWN] + back[i, 0].astype(f32) + back[i, 1].astype(f32)
        square = square + fold(g * g)
        gkv[i] = g.astype(bf16)
        c = pltpu.make_async_copy(gkv.at[i], dst, out_sem.at[1 + i])
        c.start()
        outs.append(c)

    sent = []
    value = jnp.sum(square, axis=0, keepdims=True)
    for r, (place, slots) in enumerate(((y * 8 + spot, red_a), (deep, red_b))):
        red_src[r] = value
        slots[place] = value
        copies = []
        for j, dev in enumerate(partners[r]):
            c = pltpu.make_async_remote_copy(
                src_ref=red_src.at[r],
                dst_ref=slots.at[place],
                send_sem=red_send.at[r, j],
                recv_sem=red_recv.at[r, j],
                device_id=dev,
                device_id_type=MESH,
            )
            c.start()
            copies.append(c)
        for c in copies:
            c.wait_recv()
        sent += copies
        value = jnp.sum(slots[...], axis=0)
    count = TOK * N_CTX * 8 * (GROUP + 2) * HD
    sq_out[0, 0] = jnp.sum(value) / count

    for c in sent + list(sends.values()) + returns[NEAR] + returns[FAR]:
        c.wait_send()
    for c in outs:
        c.wait()


def place_outputs(gq, gk, gv, gq_out, gk_out, gv_out, wide, narrow, sem_in, sem_out):
    parts = []
    for i, (src, dst) in enumerate(((gk, gk_out), (gv, gv_out))):
        parts.append((src, narrow.at[i], dst))
    step = TOK // 4
    for i in range(4):
        r = pl.ds(i * step, step)
        parts.append((gq.at[r], wide.at[r], gq_out.at[r]))
    first = [pltpu.make_async_copy(a, b, sem_in.at[n]) for n, (a, b, _) in enumerate(parts)]
    second = [pltpu.make_async_copy(b, c, sem_out.at[n]) for n, (_, b, c) in enumerate(parts)]
    for c in first:
        c.start()
    for a, b in zip(first, second):
        a.wait()
        b.start()
    for c in second:
        c.wait()


def shards(queries, keys, values, out_grad, outputs, block_ids):
    hbm = pl.BlockSpec(memory_space=pl.ANY)
    smem = pl.BlockSpec(memory_space=pltpu.SMEM)
    wide = GROUP * TOK
    dma = pltpu.SemaphoreType.DMA
    gq, gk, gv, square = pl.pallas_call(
        kernel,
        out_shape=(
            jax.ShapeDtypeStruct((TOK, GROUP * HD), bf16),
            jax.ShapeDtypeStruct((TOK, HD), bf16),
            jax.ShapeDtypeStruct((TOK, HD), bf16),
            jax.ShapeDtypeStruct((1, 1), f32),
        ),
        in_specs=[hbm] * 5 + [smem],
        out_specs=(hbm, hbm, hbm, smem),
        scratch_shapes=[
            pltpu.VMEM((TOK, GROUP * HD), bf16),
            pltpu.VMEM((TOK, GROUP * HD), bf16),
            pltpu.VMEM((TOK, GROUP * HD), bf16),
            pltpu.VMEM((2, 3, TOK, HD), bf16),
            pltpu.VMEM((3 * TOK, wide), f32),
            pltpu.VMEM((2 * TOK, wide), bf16),
            pltpu.VMEM((3 * TOK, wide), bf16),
            pltpu.VMEM((3 * TOK, wide), bf16),
            pltpu.VMEM((8, TOK), f32),
            pltpu.VMEM((TOK, TOK), f32),
            pltpu.VMEM((2, 3, TOK, HD), f32),
            pltpu.VMEM((TOK, GROUP * HD), bf16),
            pltpu.VMEM((2, TOK, HD), bf16),
            pltpu.VMEM((2, 2, TOK, HD), bf16),
            pltpu.VMEM((2, 2, TOK, HD), bf16),
            pltpu.VMEM((32, 1, 128), f32),
            pltpu.VMEM((16, 1, 128), f32),
            pltpu.VMEM((2, 1, 128), f32),
            dma((5,)),
            dma((3,)),
            dma((2, 3)),
            dma((2, 3)),
            dma((2, 2)),
            dma((2, 2)),
            dma((2, 31)),
            dma((2, 31)),
        ],
        compiler_params=pltpu.CompilerParams(
            collective_id=0, has_side_effects=True, vmem_limit_bytes=56 * 2**20
        ),
        name="grads",
    )(queries, keys, values, out_grad, outputs, block_ids)
    gq, gk, gv = pl.pallas_call(
        place_outputs,
        out_shape=tuple(jax.ShapeDtypeStruct(x.shape, x.dtype) for x in (gq, gk, gv)),
        in_specs=[hbm] * 3,
        out_specs=(hbm,) * 3,
        scratch_shapes=[
            pltpu.VMEM((TOK, GROUP * HD), bf16),
            pltpu.VMEM((2, TOK, HD), bf16),
            dma((6,)),
            dma((6,)),
        ],
        name="place_outputs",
    )(gq, gk, gv)
    return gq, gk, gv, square.reshape(())


def solution(mesh):
    return jax.shard_map(
        shards,
        mesh=mesh,
        in_specs=(
            P("ctx", "head"),
            P("ctx", "head"),
            P("ctx", "head"),
            P("ctx", "head"),
            P("ctx", "head"),
            P(),
        ),
        out_specs=(P("ctx", "head"), P("ctx", "head"), P("ctx", "head"), P()),
        check_vma=False,
    )
```

```python
import jax
import jax.numpy as jnp
from jax import lax
from jax.experimental import pallas as pl
from jax.experimental.pallas import tpu as pltpu
from jax.sharding import PartitionSpec as P

HD = 128
GROUP = 7
TOK = 384
BLK = 192
N_CTX = 64
SCALE = HD**-0.5
EXP2_SCALE = SCALE * 1.4426950408889634
NEG = -1e30
BIG = 1e30
HEAD_SETS = ((0, 1), (2, 3), (4, 5), (6,))
OWN, NEAR, FAR = 0, 1, 2
MESH = pl.DeviceIdType.MESH
f32 = jnp.float32
bf16 = jnp.bfloat16


def dot_nt(a, b):
    return lax.dot_general(a, b, (((1,), (1,)), ((), ())), preferred_element_type=f32)


def dot_nn(a, b):
    return lax.dot_general(a, b, (((1,), (0,)), ((), ())), preferred_element_type=f32)


def fold(x):
    rows, cols = x.shape
    y = jnp.sum(x.reshape(rows // 8, 8, cols), axis=0)
    out = y[:, :128]
    for c in range(128, cols, 128):
        out = out + y[:, c : c + 128]
    return out


def kernel(
    q_hbm, k_hbm, v_hbm, do_hbm, o_hbm, ids,
    gq_hbm, gk_hbm, gv_hbm, sq_out,
    q, do, o, kv, s, dpd, p, ds, delta, mask, acc, gq_t, gq, gkv,
    part, back, red_a, red_b, red_src,
    load_sem, out_sem, kv_send, kv_recv, part_send, part_recv, red_send, red_recv,
):
    me = lax.axis_index("ctx")
    hd = lax.axis_index("head")
    core = lax.rem(me, 2)
    near = me + 1 - 2 * core
    far = lax.rem(me + N_CTX - 1 + 2 * core, N_CTX)
    plane = me // 8
    spot = lax.rem(me, 8)
    others = {NEAR: near, FAR: far}

    y = lax.rem(hd, 4)
    deep = (hd // 4) * 8 + plane

    def across(j):
        return {"ctx": plane * 8 + lax.rem(spot + j % 8, 8), "head": hd - y + lax.rem(y + j // 8, 4)}

    def along(j):
        z = lax.rem(deep + j, 16)
        return {"ctx": lax.rem(z, 8) * 8 + spot, "head": (z // 8) * 4 + y}

    partners = [[across(j) for j in range(1, 32)], [along(j) for j in range(1, 16)]]

    barrier = pltpu.get_barrier_semaphore()
    greet = [{"ctx": far, "head": hd}, {"ctx": near, "head": hd}] + partners[0] + partners[1]
    for dev in greet:
        pl.semaphore_signal(barrier, inc=1, device_id=dev, device_id_type=MESH)
    loads = [
        pltpu.make_async_copy(src, dst, load_sem.at[i])
        for i, (src, dst) in enumerate(
            [(q_hbm, q), (k_hbm, kv.at[0, OWN]), (v_hbm, kv.at[1, OWN]), (do_hbm, do), (o_hbm, o)]
        )
    ]
    for c in loads:
        c.start()
    pl.semaphore_wait(barrier, len(greet))

    sends = {}
    for i, src in ((0, k_hbm), (1, v_hbm)):
        for side in (FAR, NEAR):
            c = pltpu.make_async_remote_copy(
                src_ref=src,
                dst_ref=kv.at[i, side],
                send_sem=kv_send.at[i, side],
                recv_sem=kv_recv.at[i, side],
                device_id={"ctx": others[side], "head": hd},
                device_id_type=MESH,
            )
            c.start()
            sends[i, side] = c

    lane = lax.broadcasted_iota(jnp.int32, (1, TOK), 1)
    row = lax.broadcasted_iota(jnp.int32, (TOK, 1), 0)
    id0, id1 = ids[2 * me], ids[2 * me + 1]
    qid = jnp.where(lane < BLK, id0, id1)
    pos_q = qid * BLK + jnp.where(lane < BLK, lane, lane - BLK)
    pos_k = jnp.where(row < BLK, id0 * BLK + row, id1 * BLK + row - BLK)
    mask[...] = jnp.where(pos_k <= pos_q, 0.0, NEG).astype(f32)
    seen = {
        side: [jnp.where(ids[2 * others[side] + b] < qid, 1, 0) for b in (0, 1)]
        for side in (NEAR, FAR)
    }

    for c in loads:
        c.wait()

    cols = lax.broadcasted_iota(jnp.int32, (TOK, HD), 1)
    gather = jnp.zeros((TOK, HD), f32)
    for h in range(GROUP):
        c = slice(h * HD, (h + 1) * HD)
        d = jnp.sum(do[:, c].astype(f32) * o[:, c].astype(f32), axis=1, keepdims=True)
        gather = jnp.where(cols == h, d, gather)
    delta[...] = gather.T[:8]

    def stack(ref, hs):
        return jnp.concatenate([ref[:, h * HD : (h + 1) * HD] for h in hs], axis=0)

    def rep(x, n):
        return jnp.concatenate([x] * n, axis=1)

    def span(hs):
        return slice(hs[0] * TOK, (hs[-1] + 1) * TOK)

    def rows(side):
        return slice(side * TOK, (side + 1) * TOK)

    peaks = {}

    def scores(side, hs):
        x = dot_nt(kv[0, side], stack(q, hs))
        if side == OWN:
            x = x + rep(mask[...], len(hs))
            peaks[side, hs] = [jnp.max(x, axis=0, keepdims=True)]
        else:
            peaks[side, hs] = [
                jnp.max(x[b * BLK : (b + 1) * BLK], axis=0, keepdims=True) for b in (0, 1)
            ]
        s[rows(side), span(hs)] = x

    def dprobs(side, hs):
        row_delta = jnp.concatenate([delta[h : h + 1] for h in hs], axis=1)
        return (dot_nt(kv[1, side], stack(do, hs)) - row_delta).astype(bf16)

    def visible(side, b, hs):
        return rep(seen[side][b], len(hs)) > 0

    def masked_probs(side, hs, m, total):
        for b in (0, 1):
            r = slice(side * TOK + b * BLK, side * TOK + (b + 1) * BLK)
            shift = jnp.where(visible(side, b, hs), m, BIG)
            e = jnp.exp2((s[r, span(hs)] - shift) * EXP2_SCALE)
            total = total + jnp.sum(e, axis=0, keepdims=True)
            p[r, span(hs)] = e.astype(bf16)
        return total

    def raised(side, hs, m):
        for b in (0, 1):
            m = jnp.maximum(m, jnp.where(visible(side, b, hs), peaks[side, hs][b], NEG))
        return m

    def columns(row, n):
        return jnp.concatenate(
            [jnp.broadcast_to(row[:, i * TOK : (i + 1) * TOK], (HD, TOK)).T for i in range(n)],
            axis=0,
        )

    def scaled(ref, hs, cols, factor):
        return (stack(ref, hs).astype(f32) * (cols * factor)).astype(bf16)

    first_stats, stats, far_scale = {}, {}, {}

    def near_part(hs):
        m = raised(NEAR, hs, peaks[OWN, hs][0])
        e = jnp.exp2((s[rows(OWN), span(hs)] - m) * EXP2_SCALE)
        total = jnp.sum(e, axis=0, keepdims=True)
        w = e.astype(bf16)
        p[rows(OWN), span(hs)] = w
        ds[rows(OWN), span(hs)] = dpd[:, span(hs)] * w
        total = masked_probs(NEAR, hs, m, total)
        ds[rows(NEAR), span(hs)] = dprobs(NEAR, hs) * p[rows(NEAR), span(hs)]
        first_stats[hs] = (m, total)

    def far_values(hs, first):
        m1, total1 = first_stats[hs]
        m = raised(FAR, hs, m1)
        f = jnp.exp2((m1 - m) * EXP2_SCALE)
        total = masked_probs(FAR, hs, m, total1 * f)
        inv = 1.0 / total
        stats[hs] = (f, inv)
        cols = columns(inv, len(hs))
        far_scale[hs] = cols
        add(1, FAR, first, dot_nn(p[rows(FAR), span(hs)], scaled(do, hs, cols, 1.0)))

    def add(i, side, first, x):
        if first:
            acc[i, side] = x
        else:
            acc[i, side] += x

    def far_keys(hs, first):
        d = dprobs(FAR, hs) * p[rows(FAR), span(hs)]
        ds[rows(FAR), span(hs)] = d
        add(0, FAR, first, dot_nn(d, scaled(q, hs, far_scale[hs], SCALE)))

    def send_back(side, i):
        part[i, side - 1] = acc[i, side].astype(bf16)
        c = pltpu.make_async_remote_copy(
            src_ref=part.at[i, side - 1],
            dst_ref=back.at[i, side - 1],
            send_sem=part_send.at[i, side - 1],
            recv_sem=part_recv.at[i, side - 1],
            device_id={"ctx": others[side], "head": hd},
            device_id_type=MESH,
        )
        c.start()
        return c

    last = len(HEAD_SETS) - 1

    for hs in HEAD_SETS:
        scores(OWN, hs)
        dpd[:, span(hs)] = dprobs(OWN, hs)
    sends[0, NEAR].wait_recv()
    sends[1, NEAR].wait_recv()
    scores(NEAR, HEAD_SETS[0])
    k_t = kv[0, 0:2].reshape(2 * TOK, HD).T
    for n, hs in enumerate(HEAD_SETS):
        if n < last:
            scores(NEAR, HEAD_SETS[n + 1])
        near_part(hs)
        gq_t[:, span(hs)] = dot_nn(k_t, ds[: 2 * TOK, span(hs)])

    sends[0, FAR].wait_recv()
    scores(FAR, HEAD_SETS[0])
    for n, hs in enumerate(HEAD_SETS):
        if n < last:
            scores(FAR, HEAD_SETS[n + 1])
        far_values(hs, n == 0)
    returns = [send_back(FAR, 1)]
    sends[1, FAR].wait_recv()
    for n, hs in enumerate(HEAD_SETS):
        far_keys(hs, n == 0)
    returns.append(send_back(FAR, 0))

    near_scale = {}
    for n, hs in enumerate(HEAD_SETS):
        f, inv = stats[hs]
        cols = columns(f * inv, len(hs))
        near_scale[hs] = (scaled(q, hs, cols, SCALE), scaled(do, hs, cols, 1.0))
        qn, don = near_scale[hs]
        add(1, NEAR, n == 0, dot_nn(p[rows(NEAR), span(hs)], don))
        add(0, NEAR, n == 0, dot_nn(ds[rows(NEAR), span(hs)], qn))
    returns += [send_back(NEAR, 1), send_back(NEAR, 0)]
    for n, hs in enumerate(HEAD_SETS):
        qn, don = near_scale[hs]
        add(1, OWN, n == 0, dot_nn(p[rows(OWN), span(hs)], don))
        add(0, OWN, n == 0, dot_nn(ds[rows(OWN), span(hs)], qn))

    square = jnp.zeros((8, 128), f32)
    far_k_t = kv[0, FAR].T
    for hs in HEAD_SETS:
        f, inv = stats[hs]
        g = dot_nn(far_k_t, ds[rows(FAR), span(hs)])
        g = (gq_t[:, span(hs)] * f + g) * (inv * SCALE)
        square = square + fold(g * g)
        for i, h in enumerate(hs):
            gq[:, h * HD : (h + 1) * HD] = g[:, i * TOK : (i + 1) * TOK].T.astype(bf16)
    outs = [pltpu.make_async_copy(gq, gq_hbm, out_sem.at[0])]
    outs[0].start()

    for c in reversed(returns):
        c.wait_recv()
    for i, dst in ((0, gk_hbm), (1, gv_hbm)):
        g = acc[i, OWN] + back[i, 0].astype(f32) + back[i, 1].astype(f32)
        square = square + fold(g * g)
        gkv[i] = g.astype(bf16)
        c = pltpu.make_async_copy(gkv.at[i], dst, out_sem.at[1 + i])
        c.start()
        outs.append(c)

    sent = []
    value = jnp.sum(square, axis=0, keepdims=True)
    for r, (place, slots) in enumerate(((y * 8 + spot, red_a), (deep, red_b))):
        red_src[r] = value
        slots[place] = value
        copies = []
        for j, dev in enumerate(partners[r]):
            c = pltpu.make_async_remote_copy(
                src_ref=red_src.at[r],
                dst_ref=slots.at[place],
                send_sem=red_send.at[r, j],
                recv_sem=red_recv.at[r, j],
                device_id=dev,
                device_id_type=MESH,
            )
            c.start()
            copies.append(c)
        for c in copies:
            c.wait_recv()
        sent += copies
        value = jnp.sum(slots[...], axis=0)
    count = TOK * N_CTX * 8 * (GROUP + 2) * HD
    sq_out[0, 0] = jnp.sum(value) / count

    for c in sent + list(sends.values()) + returns:
        c.wait_send()
    for c in outs:
        c.wait()


def place_outputs(gq, gk, gv, gq_out, gk_out, gv_out, wide, narrow, sem_in, sem_out):
    parts = []
    for i, (src, dst) in enumerate(((gk, gk_out), (gv, gv_out))):
        parts.append((src, narrow.at[i], dst))
    step = TOK // 4
    for i in range(4):
        r = pl.ds(i * step, step)
        parts.append((gq.at[r], wide.at[r], gq_out.at[r]))
    first = [pltpu.make_async_copy(a, b, sem_in.at[n]) for n, (a, b, _) in enumerate(parts)]
    second = [pltpu.make_async_copy(b, c, sem_out.at[n]) for n, (_, b, c) in enumerate(parts)]
    for c in first:
        c.start()
    for a, b in zip(first, second):
        a.wait()
        b.start()
    for c in second:
        c.wait()


def shards(queries, keys, values, out_grad, outputs, block_ids):
    hbm = pl.BlockSpec(memory_space=pl.ANY)
    smem = pl.BlockSpec(memory_space=pltpu.SMEM)
    wide = GROUP * TOK
    dma = pltpu.SemaphoreType.DMA
    gq, gk, gv, square = pl.pallas_call(
        kernel,
        out_shape=(
            jax.ShapeDtypeStruct((TOK, GROUP * HD), bf16),
            jax.ShapeDtypeStruct((TOK, HD), bf16),
            jax.ShapeDtypeStruct((TOK, HD), bf16),
            jax.ShapeDtypeStruct((1, 1), f32),
        ),
        in_specs=[hbm] * 5 + [smem],
        out_specs=(hbm, hbm, hbm, smem),
        scratch_shapes=[
            pltpu.VMEM((TOK, GROUP * HD), bf16),
            pltpu.VMEM((TOK, GROUP * HD), bf16),
            pltpu.VMEM((TOK, GROUP * HD), bf16),
            pltpu.VMEM((2, 3, TOK, HD), bf16),
            pltpu.VMEM((3 * TOK, wide), f32),
            pltpu.VMEM((TOK, wide), bf16),
            pltpu.VMEM((3 * TOK, wide), bf16),
            pltpu.VMEM((3 * TOK, wide), bf16),
            pltpu.VMEM((8, TOK), f32),
            pltpu.VMEM((TOK, TOK), f32),
            pltpu.VMEM((2, 3, TOK, HD), f32),
            pltpu.VMEM((HD, wide), f32),
            pltpu.VMEM((TOK, GROUP * HD), bf16),
            pltpu.VMEM((2, TOK, HD), bf16),
            pltpu.VMEM((2, 2, TOK, HD), bf16),
            pltpu.VMEM((2, 2, TOK, HD), bf16),
            pltpu.VMEM((32, 1, 128), f32),
            pltpu.VMEM((16, 1, 128), f32),
            pltpu.VMEM((2, 1, 128), f32),
            dma((5,)),
            dma((3,)),
            dma((2, 3)),
            dma((2, 3)),
            dma((2, 2)),
            dma((2, 2)),
            dma((2, 31)),
            dma((2, 31)),
        ],
        compiler_params=pltpu.CompilerParams(
            collective_id=0, has_side_effects=True, vmem_limit_bytes=56 * 2**20
        ),
        name="grads",
    )(queries, keys, values, out_grad, outputs, block_ids)
    gq, gk, gv = pl.pallas_call(
        place_outputs,
        out_shape=tuple(jax.ShapeDtypeStruct(x.shape, x.dtype) for x in (gq, gk, gv)),
        in_specs=[hbm] * 3,
        out_specs=(hbm,) * 3,
        scratch_shapes=[
            pltpu.VMEM((TOK, GROUP * HD), bf16),
            pltpu.VMEM((2, TOK, HD), bf16),
            dma((6,)),
            dma((6,)),
        ],
        name="place_outputs",
    )(gq, gk, gv)
    return gq, gk, gv, square.reshape(())


def solution(mesh):
    return jax.shard_map(
        shards,
        mesh=mesh,
        in_specs=(
            P("ctx", "head"),
            P("ctx", "head"),
            P("ctx", "head"),
            P("ctx", "head"),
            P("ctx", "head"),
            P(),
        ),
        out_specs=(P("ctx", "head"), P("ctx", "head"), P("ctx", "head"), P()),
        check_vma=False,
    )
```

```python
import jax
import jax.numpy as jnp
from jax import lax
from jax.experimental import pallas as pl
from jax.experimental.pallas import tpu as pltpu
from jax.sharding import PartitionSpec as P

HD = 128
GROUP = 7
TOK = 384
BLK = 192
N_CTX = 64
SCALE = HD**-0.5
EXP2_SCALE = SCALE * 1.4426950408889634
NEG = -1e30
BIG = 1e30
HEAD_SETS = ((0, 1), (2, 3), (4, 5), (6,))
OWN, NEAR, FAR = 0, 1, 2
MESH = pl.DeviceIdType.MESH
f32 = jnp.float32
bf16 = jnp.bfloat16


def dot_nt(a, b):
    return lax.dot_general(a, b, (((1,), (1,)), ((), ())), preferred_element_type=f32)


def dot_nn(a, b):
    return lax.dot_general(a, b, (((1,), (0,)), ((), ())), preferred_element_type=f32)


def fold(x):
    rows, cols = x.shape
    y = jnp.sum(x.reshape(rows // 8, 8, cols), axis=0)
    out = y[:, :128]
    for c in range(128, cols, 128):
        out = out + y[:, c : c + 128]
    return out


def kernel(
    q_hbm, k_hbm, v_hbm, do_hbm, o_hbm, ids_hbm,
    gq_hbm, gk_hbm, gv_hbm, sq_out,
    ids, q, do, o, kv, s, dpd, p, ds, delta, mask, acc, gq_t, gq, gkv,
    part, back, red_a, red_b, red_src,
    load_sem, out_sem, kv_send, kv_recv, part_send, part_recv, red_send, red_recv,
):
    me = lax.axis_index("ctx")
    hd = lax.axis_index("head")
    core = lax.rem(me, 2)
    near = me + 1 - 2 * core
    far = lax.rem(me + N_CTX - 1 + 2 * core, N_CTX)
    plane = me // 8
    spot = lax.rem(me, 8)
    others = {NEAR: near, FAR: far}

    y = lax.rem(hd, 4)
    deep = (hd // 4) * 8 + plane

    x = spot // 2

    def across(dy, dx, dc):
        there = lax.rem(x + dx, 4) * 2 + (core + dc - 2 * core * dc)
        return {"ctx": plane * 8 + there, "head": hd - y + lax.rem(y + dy, 4)}

    def along(dz):
        z = lax.rem(deep + dz, 16)
        return {"ctx": lax.rem(z, 8) * 8 + spot, "head": (z // 8) * 4 + y}

    def hops(d, n):
        return min(d, n - d)

    offsets = [(dy, dx, dc) for dy in range(4) for dx in range(4) for dc in range(2)][1:]
    offsets.sort(key=lambda d: -hops(d[0], 4) - hops(d[1], 4))
    depths = sorted(range(1, 16), key=lambda d: -hops(d, 16))
    partners = [[across(*d) for d in offsets], [along(d) for d in depths]]

    barrier = pltpu.get_barrier_semaphore()
    greet = [{"ctx": far, "head": hd}, {"ctx": near, "head": hd}] + partners[0] + partners[1]
    for dev in greet:
        pl.semaphore_signal(barrier, inc=1, device_id=dev, device_id_type=MESH)
    loads = [
        pltpu.make_async_copy(src, dst, load_sem.at[i])
        for i, (src, dst) in enumerate(
            [
                (k_hbm, kv.at[0, OWN]),
                (v_hbm, kv.at[1, OWN]),
                (ids_hbm, ids),
                (do_hbm, do),
                (o_hbm, o),
                (q_hbm, q),
            ]
        )
    ]
    for c in loads:
        c.start()
    loads[0].wait()
    loads[1].wait()
    pl.semaphore_wait(barrier, len(greet))

    sends = {}
    for i in (0, 1):
        for side in (FAR, NEAR):
            c = pltpu.make_async_remote_copy(
                src_ref=kv.at[i, OWN],
                dst_ref=kv.at[i, side],
                send_sem=kv_send.at[i, side],
                recv_sem=kv_recv.at[i, side],
                device_id={"ctx": others[side], "head": hd},
                device_id_type=MESH,
            )
            c.start()
            sends[i, side] = c

    loads[2].wait()
    lane = lax.broadcasted_iota(jnp.int32, (1, TOK), 1)
    row = lax.broadcasted_iota(jnp.int32, (TOK, 1), 0)
    id0, id1 = ids[2 * me], ids[2 * me + 1]
    qid = jnp.where(lane < BLK, id0, id1)
    pos_q = qid * BLK + jnp.where(lane < BLK, lane, lane - BLK)
    pos_k = jnp.where(row < BLK, id0 * BLK + row, id1 * BLK + row - BLK)
    mask[...] = jnp.where(pos_k <= pos_q, 0.0, NEG).astype(f32)
    seen = {
        side: [jnp.where(ids[2 * others[side] + b] < qid, 1, 0) for b in (0, 1)]
        for side in (NEAR, FAR)
    }

    for c in loads[3:]:
        c.wait()

    cols = lax.broadcasted_iota(jnp.int32, (TOK, HD), 1)
    gather = jnp.zeros((TOK, HD), f32)
    for h in range(GROUP):
        c = slice(h * HD, (h + 1) * HD)
        d = jnp.sum(do[:, c].astype(f32) * o[:, c].astype(f32), axis=1, keepdims=True)
        gather = jnp.where(cols == h, d, gather)
    delta[...] = gather.T[:8]

    def stack(ref, hs):
        return jnp.concatenate([ref[:, h * HD : (h + 1) * HD] for h in hs], axis=0)

    def rep(x, n):
        return jnp.concatenate([x] * n, axis=1)

    def span(hs):
        return slice(hs[0] * TOK, (hs[-1] + 1) * TOK)

    def rows(side):
        return slice(side * TOK, (side + 1) * TOK)

    peaks = {}

    def scores(side, hs):
        x = dot_nt(kv[0, side], stack(q, hs))
        if side == OWN:
            x = x + rep(mask[...], len(hs))
            peaks[side, hs] = [jnp.max(x, axis=0, keepdims=True)]
        else:
            peaks[side, hs] = [
                jnp.max(x[b * BLK : (b + 1) * BLK], axis=0, keepdims=True) for b in (0, 1)
            ]
        s[rows(side), span(hs)] = x

    def dprobs(side, hs):
        row_delta = jnp.concatenate([delta[h : h + 1] for h in hs], axis=1)
        return (dot_nt(kv[1, side], stack(do, hs)) - row_delta).astype(bf16)

    def visible(side, b, hs):
        return rep(seen[side][b], len(hs)) > 0

    def masked_probs(side, hs, m, total):
        for b in (0, 1):
            r = slice(side * TOK + b * BLK, side * TOK + (b + 1) * BLK)
            shift = jnp.where(visible(side, b, hs), m, BIG)
            e = jnp.exp2((s[r, span(hs)] - shift) * EXP2_SCALE)
            total = total + jnp.sum(e, axis=0, keepdims=True)
            p[r, span(hs)] = e.astype(bf16)
        return total

    def raised(side, hs, m):
        for b in (0, 1):
            m = jnp.maximum(m, jnp.where(visible(side, b, hs), peaks[side, hs][b], NEG))
        return m

    def columns(row, n):
        return jnp.concatenate(
            [jnp.broadcast_to(row[:, i * TOK : (i + 1) * TOK], (HD, TOK)).T for i in range(n)],
            axis=0,
        )

    def scaled(ref, hs, cols, factor):
        return (stack(ref, hs).astype(f32) * (cols * factor)).astype(bf16)

    first_stats, stats, far_scale = {}, {}, {}

    def near_part(hs):
        m = raised(NEAR, hs, peaks[OWN, hs][0])
        e = jnp.exp2((s[rows(OWN), span(hs)] - m) * EXP2_SCALE)
        total = jnp.sum(e, axis=0, keepdims=True)
        w = e.astype(bf16)
        p[rows(OWN), span(hs)] = w
        ds[rows(OWN), span(hs)] = dpd[:, span(hs)] * w
        total = masked_probs(NEAR, hs, m, total)
        ds[rows(NEAR), span(hs)] = dprobs(NEAR, hs) * p[rows(NEAR), span(hs)]
        first_stats[hs] = (m, total)

    def far_values(hs, first):
        m1, total1 = first_stats[hs]
        m = raised(FAR, hs, m1)
        f = jnp.exp2((m1 - m) * EXP2_SCALE)
        total = masked_probs(FAR, hs, m, total1 * f)
        inv = 1.0 / total
        stats[hs] = (f, inv)
        cols = columns(inv, len(hs))
        far_scale[hs] = cols
        add(1, FAR, first, dot_nn(p[rows(FAR), span(hs)], scaled(do, hs, cols, 1.0)))

    def add(i, side, first, x):
        if first:
            acc[i, side] = x
        else:
            acc[i, side] += x

    def far_keys(hs, first):
        d = dprobs(FAR, hs) * p[rows(FAR), span(hs)]
        ds[rows(FAR), span(hs)] = d
        add(0, FAR, first, dot_nn(d, scaled(q, hs, far_scale[hs], SCALE)))

    def send_back(side, i):
        part[i, side - 1] = acc[i, side].astype(bf16)
        c = pltpu.make_async_remote_copy(
            src_ref=part.at[i, side - 1],
            dst_ref=back.at[i, side - 1],
            send_sem=part_send.at[i, side - 1],
            recv_sem=part_recv.at[i, side - 1],
            device_id={"ctx": others[side], "head": hd},
            device_id_type=MESH,
        )
        c.start()
        return c

    last = len(HEAD_SETS) - 1

    for hs in HEAD_SETS:
        scores(OWN, hs)
        dpd[:, span(hs)] = dprobs(OWN, hs)
    sends[0, NEAR].wait_recv()
    sends[1, NEAR].wait_recv()
    scores(NEAR, HEAD_SETS[0])
    k_t = kv[0, 0:2].reshape(2 * TOK, HD).T
    for n, hs in enumerate(HEAD_SETS):
        if n < last:
            scores(NEAR, HEAD_SETS[n + 1])
        near_part(hs)
        gq_t[:, span(hs)] = dot_nn(k_t, ds[: 2 * TOK, span(hs)])

    sends[0, FAR].wait_recv()
    scores(FAR, HEAD_SETS[0])
    for n, hs in enumerate(HEAD_SETS):
        if n < last:
            scores(FAR, HEAD_SETS[n + 1])
        far_values(hs, n == 0)
    returns = [send_back(FAR, 1)]
    sends[1, FAR].wait_recv()
    for n, hs in enumerate(HEAD_SETS):
        far_keys(hs, n == 0)
    returns.append(send_back(FAR, 0))

    near_scale = {}
    for n, hs in enumerate(HEAD_SETS):
        f, inv = stats[hs]
        cols = columns(f * inv, len(hs))
        near_scale[hs] = (scaled(q, hs, cols, SCALE), scaled(do, hs, cols, 1.0))
        qn, don = near_scale[hs]
        add(1, NEAR, n == 0, dot_nn(p[rows(NEAR), span(hs)], don))
        add(0, NEAR, n == 0, dot_nn(ds[rows(NEAR), span(hs)], qn))
    returns += [send_back(NEAR, 1), send_back(NEAR, 0)]
    for n, hs in enumerate(HEAD_SETS):
        qn, don = near_scale[hs]
        add(1, OWN, n == 0, dot_nn(p[rows(OWN), span(hs)], don))
        add(0, OWN, n == 0, dot_nn(ds[rows(OWN), span(hs)], qn))

    square = jnp.zeros((8, 128), f32)
    far_k_t = kv[0, FAR].T
    for hs in HEAD_SETS:
        f, inv = stats[hs]
        g = dot_nn(far_k_t, ds[rows(FAR), span(hs)])
        g = (gq_t[:, span(hs)] * f + g) * (inv * SCALE)
        square = square + fold(g * g)
        for i, h in enumerate(hs):
            gq[:, h * HD : (h + 1) * HD] = g[:, i * TOK : (i + 1) * TOK].T.astype(bf16)
    outs = [pltpu.make_async_copy(gq, gq_hbm, out_sem.at[0])]
    outs[0].start()

    for c in reversed(returns):
        c.wait_recv()
    for i, dst in ((0, gk_hbm), (1, gv_hbm)):
        g = acc[i, OWN] + back[i, 0].astype(f32) + back[i, 1].astype(f32)
        square = square + fold(g * g)
        gkv[i] = g.astype(bf16)
        c = pltpu.make_async_copy(gkv.at[i], dst, out_sem.at[1 + i])
        c.start()
        outs.append(c)

    sent = []
    value = jnp.sum(square, axis=0, keepdims=True)
    for r, (place, slots) in enumerate(((y * 8 + spot, red_a), (deep, red_b))):
        red_src[r] = value
        slots[place] = value
        copies = []
        for j, dev in enumerate(partners[r]):
            c = pltpu.make_async_remote_copy(
                src_ref=red_src.at[r],
                dst_ref=slots.at[place],
                send_sem=red_send.at[r, j],
                recv_sem=red_recv.at[r, j],
                device_id=dev,
                device_id_type=MESH,
            )
            c.start()
            copies.append(c)
        for c in copies:
            c.wait_recv()
        sent += copies
        value = jnp.sum(slots[...], axis=0)
    count = TOK * N_CTX * 8 * (GROUP + 2) * HD
    sq_out[0, 0] = jnp.sum(value) / count

    for c in sent + list(sends.values()) + returns:
        c.wait_send()
    for c in outs:
        c.wait()


def place_outputs(gq, gk, gv, gq_out, gk_out, gv_out, wide, narrow, sem_in, sem_out):
    parts = []
    for i, (src, dst) in enumerate(((gk, gk_out), (gv, gv_out))):
        parts.append((src, narrow.at[i], dst))
    step = TOK // 4
    for i in range(4):
        r = pl.ds(i * step, step)
        parts.append((gq.at[r], wide.at[r], gq_out.at[r]))
    first = [pltpu.make_async_copy(a, b, sem_in.at[n]) for n, (a, b, _) in enumerate(parts)]
    second = [pltpu.make_async_copy(b, c, sem_out.at[n]) for n, (_, b, c) in enumerate(parts)]
    for c in first:
        c.start()
    for a, b in zip(first, second):
        a.wait()
        b.start()
    for c in second:
        c.wait()


def shards(queries, keys, values, out_grad, outputs, block_ids):
    hbm = pl.BlockSpec(memory_space=pl.ANY)
    smem = pl.BlockSpec(memory_space=pltpu.SMEM)
    wide = GROUP * TOK
    dma = pltpu.SemaphoreType.DMA
    gq, gk, gv, square = pl.pallas_call(
        kernel,
        out_shape=(
            jax.ShapeDtypeStruct((TOK, GROUP * HD), bf16),
            jax.ShapeDtypeStruct((TOK, HD), bf16),
            jax.ShapeDtypeStruct((TOK, HD), bf16),
            jax.ShapeDtypeStruct((1, 1), f32),
        ),
        in_specs=[hbm] * 6,
        out_specs=(hbm, hbm, hbm, smem),
        scratch_shapes=[
            pltpu.SMEM((2 * N_CTX,), jnp.int32),
            pltpu.VMEM((TOK, GROUP * HD), bf16),
            pltpu.VMEM((TOK, GROUP * HD), bf16),
            pltpu.VMEM((TOK, GROUP * HD), bf16),
            pltpu.VMEM((2, 3, TOK, HD), bf16),
            pltpu.VMEM((3 * TOK, wide), f32),
            pltpu.VMEM((TOK, wide), bf16),
            pltpu.VMEM((3 * TOK, wide), bf16),
            pltpu.VMEM((3 * TOK, wide), bf16),
            pltpu.VMEM((8, TOK), f32),
            pltpu.VMEM((TOK, TOK), f32),
            pltpu.VMEM((2, 3, TOK, HD), f32),
            pltpu.VMEM((HD, wide), f32),
            pltpu.VMEM((TOK, GROUP * HD), bf16),
            pltpu.VMEM((2, TOK, HD), bf16),
            pltpu.VMEM((2, 2, TOK, HD), bf16),
            pltpu.VMEM((2, 2, TOK, HD), bf16),
            pltpu.VMEM((32, 1, 128), f32),
            pltpu.VMEM((16, 1, 128), f32),
            pltpu.VMEM((2, 1, 128), f32),
            dma((6,)),
            dma((3,)),
            dma((2, 3)),
            dma((2, 3)),
            dma((2, 2)),
            dma((2, 2)),
            dma((2, 31)),
            dma((2, 31)),
        ],
        compiler_params=pltpu.CompilerParams(
            collective_id=0, has_side_effects=True, vmem_limit_bytes=56 * 2**20
        ),
        name="grads",
    )(queries, keys, values, out_grad, outputs, block_ids)
    gq, gk, gv = pl.pallas_call(
        place_outputs,
        out_shape=tuple(jax.ShapeDtypeStruct(x.shape, x.dtype) for x in (gq, gk, gv)),
        in_specs=[hbm] * 3,
        out_specs=(hbm,) * 3,
        scratch_shapes=[
            pltpu.VMEM((TOK, GROUP * HD), bf16),
            pltpu.VMEM((2, TOK, HD), bf16),
            dma((6,)),
            dma((6,)),
        ],
        name="place_outputs",
    )(gq, gk, gv)
    return gq, gk, gv, square.reshape(())


def solution(mesh):
    return jax.shard_map(
        shards,
        mesh=mesh,
        in_specs=(
            P("ctx", "head"),
            P("ctx", "head"),
            P("ctx", "head"),
            P("ctx", "head"),
            P("ctx", "head"),
            P(),
        ),
        out_specs=(P("ctx", "head"), P("ctx", "head"), P("ctx", "head"), P()),
        check_vma=False,
    )
```

```python
import jax
import jax.numpy as jnp
from jax import lax
from jax.experimental import pallas as pl
from jax.experimental.pallas import tpu as pltpu
from jax.sharding import PartitionSpec as P

HD = 128
GROUP = 7
TOK = 384
BLK = 192
N_CTX = 64
SCALE = HD**-0.5
EXP2_SCALE = SCALE * 1.4426950408889634
NEG = -1e30
BIG = 1e30
HEAD_SETS = ((0, 1), (2, 3), (4, 5), (6,))
OWN, NEAR, FAR = 0, 1, 2
MESH = pl.DeviceIdType.MESH
f32 = jnp.float32
bf16 = jnp.bfloat16


def dot_nt(a, b):
    return lax.dot_general(a, b, (((1,), (1,)), ((), ())), preferred_element_type=f32)


def dot_nn(a, b):
    return lax.dot_general(a, b, (((1,), (0,)), ((), ())), preferred_element_type=f32)


def fold(x):
    rows, cols = x.shape
    y = jnp.sum(x.reshape(rows // 8, 8, cols), axis=0)
    out = y[:, :128]
    for c in range(128, cols, 128):
        out = out + y[:, c : c + 128]
    return out


def kernel(
    q_hbm, k_hbm, v_hbm, do_hbm, o_hbm, ids_hbm,
    gq_hbm, gk_hbm, gv_hbm, sq_out,
    ids, q, do, o, kv, s, dpd, p, ds, delta, mask, acc, gq_t, gq, gkv,
    part, back, red_a, red_b, red_src,
    load_sem, out_sem, kv_send, kv_recv, part_send, part_recv, red_send, red_recv,
):
    me = lax.axis_index("ctx")
    hd = lax.axis_index("head")
    core = lax.rem(me, 2)
    near = me + 1 - 2 * core
    far = lax.rem(me + N_CTX - 1 + 2 * core, N_CTX)
    plane = me // 8
    spot = lax.rem(me, 8)
    others = {NEAR: near, FAR: far}

    y = lax.rem(hd, 4)
    deep = (hd // 4) * 8 + plane

    x = spot // 2

    def across(dy, dx, dc):
        there = lax.rem(x + dx, 4) * 2 + (core + dc - 2 * core * dc)
        return {"ctx": plane * 8 + there, "head": hd - y + lax.rem(y + dy, 4)}

    def along(dz):
        z = lax.rem(deep + dz, 16)
        return {"ctx": lax.rem(z, 8) * 8 + spot, "head": (z // 8) * 4 + y}

    def hops(d, n):
        return min(d, n - d)

    offsets = [(dy, dx, dc) for dy in range(4) for dx in range(4) for dc in range(2)][1:]
    offsets.sort(key=lambda d: -hops(d[0], 4) - hops(d[1], 4))
    depths = sorted(range(1, 16), key=lambda d: -hops(d, 16))
    partners = [[across(*d) for d in offsets], [along(d) for d in depths]]

    barrier = pltpu.get_barrier_semaphore()
    greet = [{"ctx": far, "head": hd}, {"ctx": near, "head": hd}] + partners[0] + partners[1]
    for dev in greet:
        pl.semaphore_signal(barrier, inc=1, device_id=dev, device_id_type=MESH)
    loads = [
        pltpu.make_async_copy(src, dst, load_sem.at[i])
        for i, (src, dst) in enumerate(
            [
                (k_hbm, kv.at[0, OWN]),
                (v_hbm, kv.at[1, OWN]),
                (ids_hbm, ids),
                (do_hbm, do),
                (o_hbm, o),
                (q_hbm, q),
            ]
        )
    ]
    for c in loads:
        c.start()
    loads[2].wait()
    lane = lax.broadcasted_iota(jnp.int32, (1, TOK), 1)
    row = lax.broadcasted_iota(jnp.int32, (TOK, 1), 0)
    id0, id1 = ids[2 * me], ids[2 * me + 1]
    qid = jnp.where(lane < BLK, id0, id1)
    pos_q = qid * BLK + jnp.where(lane < BLK, lane, lane - BLK)
    pos_k = jnp.where(row < BLK, id0 * BLK + row, id1 * BLK + row - BLK)
    mask[...] = jnp.where(pos_k <= pos_q, 0.0, NEG).astype(f32)
    seen = {
        side: [jnp.where(ids[2 * others[side] + b] < qid, 1, 0) for b in (0, 1)]
        for side in (NEAR, FAR)
    }

    for c in loads[3:]:
        c.wait()

    cols = lax.broadcasted_iota(jnp.int32, (TOK, HD), 1)
    gather = jnp.zeros((TOK, HD), f32)
    for h in range(GROUP):
        c = slice(h * HD, (h + 1) * HD)
        d = jnp.sum(do[:, c].astype(f32) * o[:, c].astype(f32), axis=1, keepdims=True)
        gather = jnp.where(cols == h, d, gather)
    delta[...] = gather.T[:8]

    def stack(ref, hs):
        return jnp.concatenate([ref[:, h * HD : (h + 1) * HD] for h in hs], axis=0)

    def rep(x, n):
        return jnp.concatenate([x] * n, axis=1)

    def span(hs):
        return slice(hs[0] * TOK, (hs[-1] + 1) * TOK)

    def rows(side):
        return slice(side * TOK, (side + 1) * TOK)

    peaks = {}

    def scores(side, hs):
        x = dot_nt(kv[0, side], stack(q, hs))
        if side == OWN:
            x = x + rep(mask[...], len(hs))
            peaks[side, hs] = [jnp.max(x, axis=0, keepdims=True)]
        else:
            peaks[side, hs] = [
                jnp.max(x[b * BLK : (b + 1) * BLK], axis=0, keepdims=True) for b in (0, 1)
            ]
        s[rows(side), span(hs)] = x

    def dprobs(side, hs):
        row_delta = jnp.concatenate([delta[h : h + 1] for h in hs], axis=1)
        return (dot_nt(kv[1, side], stack(do, hs)) - row_delta).astype(bf16)

    def visible(side, b, hs):
        return rep(seen[side][b], len(hs)) > 0

    def masked_probs(side, hs, m, total):
        for b in (0, 1):
            r = slice(side * TOK + b * BLK, side * TOK + (b + 1) * BLK)
            shift = jnp.where(visible(side, b, hs), m, BIG)
            e = jnp.exp2((s[r, span(hs)] - shift) * EXP2_SCALE)
            total = total + jnp.sum(e, axis=0, keepdims=True)
            p[r, span(hs)] = e.astype(bf16)
        return total

    def raised(side, hs, m):
        for b in (0, 1):
            m = jnp.maximum(m, jnp.where(visible(side, b, hs), peaks[side, hs][b], NEG))
        return m

    def columns(row, n):
        return jnp.concatenate(
            [jnp.broadcast_to(row[:, i * TOK : (i + 1) * TOK], (HD, TOK)).T for i in range(n)],
            axis=0,
        )

    def scaled(ref, hs, cols, factor):
        return (stack(ref, hs).astype(f32) * (cols * factor)).astype(bf16)

    first_stats, stats, far_scale = {}, {}, {}

    def near_part(hs):
        m = raised(NEAR, hs, peaks[OWN, hs][0])
        e = jnp.exp2((s[rows(OWN), span(hs)] - m) * EXP2_SCALE)
        total = jnp.sum(e, axis=0, keepdims=True)
        w = e.astype(bf16)
        p[rows(OWN), span(hs)] = w
        ds[rows(OWN), span(hs)] = dpd[:, span(hs)] * w
        total = masked_probs(NEAR, hs, m, total)
        ds[rows(NEAR), span(hs)] = dprobs(NEAR, hs) * p[rows(NEAR), span(hs)]
        first_stats[hs] = (m, total)

    def far_values(hs, first):
        m1, total1 = first_stats[hs]
        m = raised(FAR, hs, m1)
        f = jnp.exp2((m1 - m) * EXP2_SCALE)
        total = masked_probs(FAR, hs, m, total1 * f)
        inv = 1.0 / total
        stats[hs] = (f, inv)
        cols = columns(inv, len(hs))
        far_scale[hs] = cols
        add(1, FAR, first, dot_nn(p[rows(FAR), span(hs)], scaled(do, hs, cols, 1.0)))

    def add(i, side, first, x):
        if first:
            acc[i, side] = x
        else:
            acc[i, side] += x

    def far_keys(hs, first):
        d = dprobs(FAR, hs) * p[rows(FAR), span(hs)]
        ds[rows(FAR), span(hs)] = d
        add(0, FAR, first, dot_nn(d, scaled(q, hs, far_scale[hs], SCALE)))

    def send_back(side, i):
        part[i, side - 1] = acc[i, side].astype(bf16)
        c = pltpu.make_async_remote_copy(
            src_ref=part.at[i, side - 1],
            dst_ref=back.at[i, side - 1],
            send_sem=part_send.at[i, side - 1],
            recv_sem=part_recv.at[i, side - 1],
            device_id={"ctx": others[side], "head": hd},
            device_id_type=MESH,
        )
        c.start()
        return c

    last = len(HEAD_SETS) - 1

    loads[0].wait()
    loads[1].wait()
    for hs in HEAD_SETS:
        scores(OWN, hs)
        dpd[:, span(hs)] = dprobs(OWN, hs)
    pl.semaphore_wait(barrier, len(greet))

    sends = {}
    for i in (0, 1):
        for side in (FAR, NEAR):
            c = pltpu.make_async_remote_copy(
                src_ref=kv.at[i, OWN],
                dst_ref=kv.at[i, side],
                send_sem=kv_send.at[i, side],
                recv_sem=kv_recv.at[i, side],
                device_id={"ctx": others[side], "head": hd},
                device_id_type=MESH,
            )
            c.start()
            sends[i, side] = c

    sends[0, NEAR].wait_recv()
    sends[1, NEAR].wait_recv()
    scores(NEAR, HEAD_SETS[0])
    k_t = kv[0, 0:2].reshape(2 * TOK, HD).T
    for n, hs in enumerate(HEAD_SETS):
        if n < last:
            scores(NEAR, HEAD_SETS[n + 1])
        near_part(hs)
        gq_t[:, span(hs)] = dot_nn(k_t, ds[: 2 * TOK, span(hs)])

    sends[0, FAR].wait_recv()
    scores(FAR, HEAD_SETS[0])
    for n, hs in enumerate(HEAD_SETS):
        if n < last:
            scores(FAR, HEAD_SETS[n + 1])
        far_values(hs, n == 0)
    returns = [send_back(FAR, 1)]
    sends[1, FAR].wait_recv()
    for n, hs in enumerate(HEAD_SETS):
        far_keys(hs, n == 0)
    returns.append(send_back(FAR, 0))

    near_scale = {}
    for n, hs in enumerate(HEAD_SETS):
        f, inv = stats[hs]
        cols = columns(f * inv, len(hs))
        near_scale[hs] = (scaled(q, hs, cols, SCALE), scaled(do, hs, cols, 1.0))
        qn, don = near_scale[hs]
        add(1, NEAR, n == 0, dot_nn(p[rows(NEAR), span(hs)], don))
        add(0, NEAR, n == 0, dot_nn(ds[rows(NEAR), span(hs)], qn))
    returns += [send_back(NEAR, 1), send_back(NEAR, 0)]
    for n, hs in enumerate(HEAD_SETS):
        qn, don = near_scale[hs]
        add(1, OWN, n == 0, dot_nn(p[rows(OWN), span(hs)], don))
        add(0, OWN, n == 0, dot_nn(ds[rows(OWN), span(hs)], qn))

    square = jnp.zeros((8, 128), f32)
    far_k_t = kv[0, FAR].T
    for hs in HEAD_SETS:
        f, inv = stats[hs]
        g = dot_nn(far_k_t, ds[rows(FAR), span(hs)])
        g = (gq_t[:, span(hs)] * f + g) * (inv * SCALE)
        square = square + fold(g * g)
        for i, h in enumerate(hs):
            gq[:, h * HD : (h + 1) * HD] = g[:, i * TOK : (i + 1) * TOK].T.astype(bf16)
    outs = [pltpu.make_async_copy(gq, gq_hbm, out_sem.at[0])]
    outs[0].start()

    for i, dst, arrivals in ((1, gv_hbm, (2, 0)), (0, gk_hbm, (3, 1))):
        for n in arrivals:
            returns[n].wait_recv()
        g = acc[i, OWN] + back[i, 0].astype(f32) + back[i, 1].astype(f32)
        square = square + fold(g * g)
        gkv[i] = g.astype(bf16)
        c = pltpu.make_async_copy(gkv.at[i], dst, out_sem.at[1 + i])
        c.start()
        outs.append(c)

    value = jnp.sum(square, axis=0, keepdims=True)
    for r, (place, slots) in enumerate(((y * 8 + spot, red_a), (deep, red_b))):
        red_src[r] = value
        slots[place] = value
        copies = []
        for j, dev in enumerate(partners[r]):
            c = pltpu.make_async_remote_copy(
                src_ref=red_src.at[r],
                dst_ref=slots.at[place],
                send_sem=red_send.at[r, j],
                recv_sem=red_recv.at[r, j],
                device_id=dev,
                device_id_type=MESH,
            )
            c.start()
            copies.append(c)
        if r == 0:
            for c in list(sends.values()) + returns:
                c.wait_send()
        else:
            for c in outs:
                c.wait()
        for c in copies:
            c.wait_send()
        for c in reversed(copies):
            c.wait_recv()
        value = jnp.sum(slots[...], axis=0)
    count = TOK * N_CTX * 8 * (GROUP + 2) * HD
    sq_out[0, 0] = jnp.sum(value) / count


def place_outputs(gq, gk, gv, gq_out, gk_out, gv_out, wide, narrow, sem_in, sem_out):
    parts = []
    for i, (src, dst) in enumerate(((gk, gk_out), (gv, gv_out))):
        parts.append((src, narrow.at[i], dst))
    step = TOK // 4
    for i in range(4):
        r = pl.ds(i * step, step)
        parts.append((gq.at[r], wide.at[r], gq_out.at[r]))
    first = [pltpu.make_async_copy(a, b, sem_in.at[n]) for n, (a, b, _) in enumerate(parts)]
    second = [pltpu.make_async_copy(b, c, sem_out.at[n]) for n, (_, b, c) in enumerate(parts)]
    for c in first:
        c.start()
    for a, b in zip(first, second):
        a.wait()
        b.start()
    for c in second:
        c.wait()


def shards(queries, keys, values, out_grad, outputs, block_ids):
    hbm = pl.BlockSpec(memory_space=pl.ANY)
    smem = pl.BlockSpec(memory_space=pltpu.SMEM)
    wide = GROUP * TOK
    dma = pltpu.SemaphoreType.DMA
    gq, gk, gv, square = pl.pallas_call(
        kernel,
        out_shape=(
            jax.ShapeDtypeStruct((TOK, GROUP * HD), bf16),
            jax.ShapeDtypeStruct((TOK, HD), bf16),
            jax.ShapeDtypeStruct((TOK, HD), bf16),
            jax.ShapeDtypeStruct((1, 1), f32),
        ),
        in_specs=[hbm] * 6,
        out_specs=(hbm, hbm, hbm, smem),
        scratch_shapes=[
            pltpu.SMEM((2 * N_CTX,), jnp.int32),
            pltpu.VMEM((TOK, GROUP * HD), bf16),
            pltpu.VMEM((TOK, GROUP * HD), bf16),
            pltpu.VMEM((TOK, GROUP * HD), bf16),
            pltpu.VMEM((2, 3, TOK, HD), bf16),
            pltpu.VMEM((3 * TOK, wide), f32),
            pltpu.VMEM((TOK, wide), bf16),
            pltpu.VMEM((3 * TOK, wide), bf16),
            pltpu.VMEM((3 * TOK, wide), bf16),
            pltpu.VMEM((8, TOK), f32),
            pltpu.VMEM((TOK, TOK), f32),
            pltpu.VMEM((2, 3, TOK, HD), f32),
            pltpu.VMEM((HD, wide), f32),
            pltpu.VMEM((TOK, GROUP * HD), bf16),
            pltpu.VMEM((2, TOK, HD), bf16),
            pltpu.VMEM((2, 2, TOK, HD), bf16),
            pltpu.VMEM((2, 2, TOK, HD), bf16),
            pltpu.VMEM((32, 1, 128), f32),
            pltpu.VMEM((16, 1, 128), f32),
            pltpu.VMEM((2, 1, 128), f32),
            dma((6,)),
            dma((3,)),
            dma((2, 3)),
            dma((2, 3)),
            dma((2, 2)),
            dma((2, 2)),
            dma((2, 31)),
            dma((2, 31)),
        ],
        compiler_params=pltpu.CompilerParams(
            collective_id=0, has_side_effects=True, vmem_limit_bytes=56 * 2**20
        ),
        name="grads",
    )(queries, keys, values, out_grad, outputs, block_ids)
    gq, gk, gv = pl.pallas_call(
        place_outputs,
        out_shape=tuple(jax.ShapeDtypeStruct(x.shape, x.dtype) for x in (gq, gk, gv)),
        in_specs=[hbm] * 3,
        out_specs=(hbm,) * 3,
        scratch_shapes=[
            pltpu.VMEM((TOK, GROUP * HD), bf16),
            pltpu.VMEM((2, TOK, HD), bf16),
            dma((6,)),
            dma((6,)),
        ],
        name="place_outputs",
    )(gq, gk, gv)
    return gq, gk, gv, square.reshape(())


def solution(mesh):
    return jax.shard_map(
        shards,
        mesh=mesh,
        in_specs=(
            P("ctx", "head"),
            P("ctx", "head"),
            P("ctx", "head"),
            P("ctx", "head"),
            P("ctx", "head"),
            P(),
        ),
        out_specs=(P("ctx", "head"), P("ctx", "head"), P("ctx", "head"), P()),
        check_vma=False,
    )
```

```python
import jax
import jax.numpy as jnp
from jax import lax
from jax.experimental import pallas as pl
from jax.experimental.pallas import tpu as pltpu
from jax.sharding import PartitionSpec as P

HD = 128
GROUP = 7
TOK = 384
BLK = 192
N_CTX = 64
SCALE = HD**-0.5
EXP2_SCALE = SCALE * 1.4426950408889634
NEG = -1e30
BIG = 1e30
HEAD_SETS = ((0, 1), (2, 3), (4, 5), (6,))
OWN, NEAR, FAR = 0, 1, 2
MESH = pl.DeviceIdType.MESH
f32 = jnp.float32
bf16 = jnp.bfloat16


def dot_nt(a, b):
    return lax.dot_general(a, b, (((1,), (1,)), ((), ())), preferred_element_type=f32)


def dot_nn(a, b):
    return lax.dot_general(a, b, (((1,), (0,)), ((), ())), preferred_element_type=f32)


def fold(x):
    rows, cols = x.shape
    y = jnp.sum(x.reshape(rows // 8, 8, cols), axis=0)
    out = y[:, :128]
    for c in range(128, cols, 128):
        out = out + y[:, c : c + 128]
    return out


def kernel(
    q_hbm, k_hbm, v_hbm, do_hbm, o_hbm, ids_hbm,
    gq_hbm, gk_hbm, gv_hbm, sq_out,
    ids, q, do, o, kv, s, dpd, p, ds, delta, mask, acc, gq_t, gq, gkv,
    part, back, red_a, red_b, red_src,
    load_sem, out_sem, kv_send, kv_recv, part_send, part_recv, red_send, red_recv,
):
    me = lax.axis_index("ctx")
    hd = lax.axis_index("head")
    core = lax.rem(me, 2)
    near = me + 1 - 2 * core
    far = lax.rem(me + N_CTX - 1 + 2 * core, N_CTX)
    plane = me // 8
    spot = lax.rem(me, 8)
    others = {NEAR: near, FAR: far}

    y = lax.rem(hd, 4)
    deep = (hd // 4) * 8 + plane

    x = spot // 2

    def across(dy, dx, dc):
        there = lax.rem(x + dx, 4) * 2 + (core + dc - 2 * core * dc)
        return {"ctx": plane * 8 + there, "head": hd - y + lax.rem(y + dy, 4)}

    def along(dz):
        z = lax.rem(deep + dz, 16)
        return {"ctx": lax.rem(z, 8) * 8 + spot, "head": (z // 8) * 4 + y}

    def hops(d, n):
        return min(d, n - d)

    offsets = [(dy, dx, dc) for dy in range(4) for dx in range(4) for dc in range(2)][1:]
    offsets.sort(key=lambda d: -hops(d[0], 4) - hops(d[1], 4))
    depths = sorted(range(1, 16), key=lambda d: -hops(d, 16))
    partners = [[across(*d) for d in offsets], [along(d) for d in depths]]

    barrier = pltpu.get_barrier_semaphore()
    greet = [{"ctx": far, "head": hd}, {"ctx": near, "head": hd}] + partners[0] + partners[1]
    for dev in greet:
        pl.semaphore_signal(barrier, inc=1, device_id=dev, device_id_type=MESH)
    loads = [
        pltpu.make_async_copy(src, dst, load_sem.at[i])
        for i, (src, dst) in enumerate(
            [
                (k_hbm, kv.at[0, OWN]),
                (v_hbm, kv.at[1, OWN]),
                (ids_hbm, ids),
                (do_hbm, do),
                (o_hbm, o),
                (q_hbm, q),
            ]
        )
    ]
    for c in loads:
        c.start()
    loads[2].wait()
    lane = lax.broadcasted_iota(jnp.int32, (1, TOK), 1)
    row = lax.broadcasted_iota(jnp.int32, (TOK, 1), 0)
    id0, id1 = ids[2 * me], ids[2 * me + 1]
    qid = jnp.where(lane < BLK, id0, id1)
    pos_q = qid * BLK + jnp.where(lane < BLK, lane, lane - BLK)
    pos_k = jnp.where(row < BLK, id0 * BLK + row, id1 * BLK + row - BLK)
    mask[...] = jnp.where(pos_k <= pos_q, 0.0, NEG).astype(f32)
    seen = {
        side: [jnp.where(ids[2 * others[side] + b] < qid, 1, 0) for b in (0, 1)]
        for side in (NEAR, FAR)
    }

    for c in loads[3:]:
        c.wait()

    cols = lax.broadcasted_iota(jnp.int32, (TOK, HD), 1)
    gather = jnp.zeros((TOK, HD), f32)
    for h in range(GROUP):
        c = slice(h * HD, (h + 1) * HD)
        d = jnp.sum(do[:, c].astype(f32) * o[:, c].astype(f32), axis=1, keepdims=True)
        gather = jnp.where(cols == h, d, gather)
    delta[...] = gather.T[:8]

    def stack(ref, hs):
        return jnp.concatenate([ref[:, h * HD : (h + 1) * HD] for h in hs], axis=0)

    def rep(x, n):
        return jnp.concatenate([x] * n, axis=1)

    def span(hs):
        return slice(hs[0] * TOK, (hs[-1] + 1) * TOK)

    def rows(side):
        return slice(side * TOK, (side + 1) * TOK)

    peaks = {}

    def scores(side, hs):
        x = dot_nt(kv[0, side], stack(q, hs))
        if side == OWN:
            x = x + rep(mask[...], len(hs))
            peaks[side, hs] = [jnp.max(x, axis=0, keepdims=True)]
        else:
            peaks[side, hs] = [
                jnp.max(x[b * BLK : (b + 1) * BLK], axis=0, keepdims=True) for b in (0, 1)
            ]
        s[rows(side), span(hs)] = x

    def dprobs(side, hs):
        row_delta = jnp.concatenate([delta[h : h + 1] for h in hs], axis=1)
        return (dot_nt(kv[1, side], stack(do, hs)) - row_delta).astype(bf16)

    def visible(side, b, hs):
        return rep(seen[side][b], len(hs)) > 0

    def masked_probs(side, hs, m, total):
        for b in (0, 1):
            r = slice(side * TOK + b * BLK, side * TOK + (b + 1) * BLK)
            shift = jnp.where(visible(side, b, hs), m, BIG)
            e = jnp.exp2((s[r, span(hs)] - shift) * EXP2_SCALE)
            total = total + jnp.sum(e, axis=0, keepdims=True)
            p[r, span(hs)] = e.astype(bf16)
        return total

    def raised(side, hs, m):
        for b in (0, 1):
            m = jnp.maximum(m, jnp.where(visible(side, b, hs), peaks[side, hs][b], NEG))
        return m

    def columns(row, n):
        return jnp.concatenate(
            [jnp.broadcast_to(row[:, i * TOK : (i + 1) * TOK], (HD, TOK)).T for i in range(n)],
            axis=0,
        )

    def scaled(ref, hs, cols, factor):
        return (stack(ref, hs).astype(f32) * (cols * factor)).astype(bf16)

    first_stats, stats, far_scale = {}, {}, {}

    def near_part(hs):
        m = raised(NEAR, hs, peaks[OWN, hs][0])
        e = jnp.exp2((s[rows(OWN), span(hs)] - m) * EXP2_SCALE)
        total = jnp.sum(e, axis=0, keepdims=True)
        w = e.astype(bf16)
        p[rows(OWN), span(hs)] = w
        ds[rows(OWN), span(hs)] = dpd[:, span(hs)] * w
        total = masked_probs(NEAR, hs, m, total)
        ds[rows(NEAR), span(hs)] = dprobs(NEAR, hs) * p[rows(NEAR), span(hs)]
        first_stats[hs] = (m, total)

    def far_values(hs, first):
        m1, total1 = first_stats[hs]
        m = raised(FAR, hs, m1)
        f = jnp.exp2((m1 - m) * EXP2_SCALE)
        total = masked_probs(FAR, hs, m, total1 * f)
        inv = 1.0 / total
        stats[hs] = (f, inv)
        cols = columns(inv, len(hs))
        far_scale[hs] = cols
        add(1, FAR, first, dot_nn(p[rows(FAR), span(hs)], scaled(do, hs, cols, 1.0)))

    def add(i, side, first, x):
        if first:
            acc[i, side] = x
        else:
            acc[i, side] += x

    def far_keys(hs, first):
        d = dprobs(FAR, hs) * p[rows(FAR), span(hs)]
        ds[rows(FAR), span(hs)] = d
        add(0, FAR, first, dot_nn(d, scaled(q, hs, far_scale[hs], SCALE)))

    def send_back(side, i):
        part[i, side - 1] = acc[i, side].astype(bf16)
        c = pltpu.make_async_remote_copy(
            src_ref=part.at[i, side - 1],
            dst_ref=back.at[i, side - 1],
            send_sem=part_send.at[i, side - 1],
            recv_sem=part_recv.at[i, side - 1],
            device_id={"ctx": others[side], "head": hd},
            device_id_type=MESH,
        )
        c.start()
        return c

    last = len(HEAD_SETS) - 1

    loads[0].wait()
    loads[1].wait()
    for hs in HEAD_SETS:
        scores(OWN, hs)
        dpd[:, span(hs)] = dprobs(OWN, hs)
    pl.semaphore_wait(barrier, len(greet))

    sends = {}
    for side in (FAR, NEAR):
        for i in (0, 1):
            c = pltpu.make_async_remote_copy(
                src_ref=kv.at[i, OWN],
                dst_ref=kv.at[i, side],
                send_sem=kv_send.at[i, side],
                recv_sem=kv_recv.at[i, side],
                device_id={"ctx": others[side], "head": hd},
                device_id_type=MESH,
            )
            c.start()
            sends[i, side] = c

    sends[0, NEAR].wait_recv()
    sends[1, NEAR].wait_recv()
    scores(NEAR, HEAD_SETS[0])
    k_t = kv[0, 0:2].reshape(2 * TOK, HD).T
    for n, hs in enumerate(HEAD_SETS):
        if n < last:
            scores(NEAR, HEAD_SETS[n + 1])
        near_part(hs)
        gq_t[:, span(hs)] = dot_nn(k_t, ds[: 2 * TOK, span(hs)])

    sends[0, FAR].wait_recv()
    scores(FAR, HEAD_SETS[0])
    for n, hs in enumerate(HEAD_SETS):
        if n < last:
            scores(FAR, HEAD_SETS[n + 1])
        far_values(hs, n == 0)
    returns = [send_back(FAR, 1)]
    sends[1, FAR].wait_recv()
    for n, hs in enumerate(HEAD_SETS):
        far_keys(hs, n == 0)
    returns.append(send_back(FAR, 0))

    near_scale = {}
    for n, hs in enumerate(HEAD_SETS):
        f, inv = stats[hs]
        cols = columns(f * inv, len(hs))
        near_scale[hs] = (scaled(q, hs, cols, SCALE), scaled(do, hs, cols, 1.0))
        qn, don = near_scale[hs]
        add(1, NEAR, n == 0, dot_nn(p[rows(NEAR), span(hs)], don))
        add(0, NEAR, n == 0, dot_nn(ds[rows(NEAR), span(hs)], qn))
    returns += [send_back(NEAR, 1), send_back(NEAR, 0)]
    for n, hs in enumerate(HEAD_SETS):
        qn, don = near_scale[hs]
        add(1, OWN, n == 0, dot_nn(p[rows(OWN), span(hs)], don))
        add(0, OWN, n == 0, dot_nn(ds[rows(OWN), span(hs)], qn))

    square = jnp.zeros((8, 128), f32)
    far_k_t = kv[0, FAR].T
    for hs in HEAD_SETS:
        f, inv = stats[hs]
        g = dot_nn(far_k_t, ds[rows(FAR), span(hs)])
        g = (gq_t[:, span(hs)] * f + g) * (inv * SCALE)
        square = square + fold(g * g)
        for i, h in enumerate(hs):
            gq[:, h * HD : (h + 1) * HD] = g[:, i * TOK : (i + 1) * TOK].T.astype(bf16)
    outs = [pltpu.make_async_copy(gq, gq_hbm, out_sem.at[0])]
    outs[0].start()

    for i, dst, arrivals in ((1, gv_hbm, (2, 0)), (0, gk_hbm, (3, 1))):
        for n in arrivals:
            returns[n].wait_recv()
        g = acc[i, OWN] + back[i, 0].astype(f32) + back[i, 1].astype(f32)
        square = square + fold(g * g)
        gkv[i] = g.astype(bf16)
        c = pltpu.make_async_copy(gkv.at[i], dst, out_sem.at[1 + i])
        c.start()
        outs.append(c)

    value = jnp.sum(square, axis=0, keepdims=True)
    for r, (place, slots) in enumerate(((y * 8 + spot, red_a), (deep, red_b))):
        red_src[r] = value
        slots[place] = value
        copies = []
        for j, dev in enumerate(partners[r]):
            c = pltpu.make_async_remote_copy(
                src_ref=red_src.at[r],
                dst_ref=slots.at[place],
                send_sem=red_send.at[r, j],
                recv_sem=red_recv.at[r, j],
                device_id=dev,
                device_id_type=MESH,
            )
            c.start()
            copies.append(c)
        if r == 0:
            for c in list(sends.values()) + returns:
                c.wait_send()
        else:
            for c in outs:
                c.wait()
        for c in copies:
            c.wait_send()
        for c in reversed(copies):
            c.wait_recv()
        value = jnp.sum(slots[...], axis=0)
    count = TOK * N_CTX * 8 * (GROUP + 2) * HD
    sq_out[0, 0] = jnp.sum(value) / count


def place_outputs(gq, gk, gv, gq_out, gk_out, gv_out, wide, narrow, sem_in, sem_out):
    parts = []
    for i, (src, dst) in enumerate(((gk, gk_out), (gv, gv_out))):
        parts.append((src, narrow.at[i], dst))
    step = TOK // 4
    for i in range(4):
        r = pl.ds(i * step, step)
        parts.append((gq.at[r], wide.at[r], gq_out.at[r]))
    first = [pltpu.make_async_copy(a, b, sem_in.at[n]) for n, (a, b, _) in enumerate(parts)]
    second = [pltpu.make_async_copy(b, c, sem_out.at[n]) for n, (_, b, c) in enumerate(parts)]
    for c in first:
        c.start()
    for a, b in zip(first, second):
        a.wait()
        b.start()
    for c in second:
        c.wait()


def shards(queries, keys, values, out_grad, outputs, block_ids):
    hbm = pl.BlockSpec(memory_space=pl.ANY)
    smem = pl.BlockSpec(memory_space=pltpu.SMEM)
    wide = GROUP * TOK
    dma = pltpu.SemaphoreType.DMA
    gq, gk, gv, square = pl.pallas_call(
        kernel,
        out_shape=(
            jax.ShapeDtypeStruct((TOK, GROUP * HD), bf16),
            jax.ShapeDtypeStruct((TOK, HD), bf16),
            jax.ShapeDtypeStruct((TOK, HD), bf16),
            jax.ShapeDtypeStruct((1, 1), f32),
        ),
        in_specs=[hbm] * 6,
        out_specs=(hbm, hbm, hbm, smem),
        scratch_shapes=[
            pltpu.SMEM((2 * N_CTX,), jnp.int32),
            pltpu.VMEM((TOK, GROUP * HD), bf16),
            pltpu.VMEM((TOK, GROUP * HD), bf16),
            pltpu.VMEM((TOK, GROUP * HD), bf16),
            pltpu.VMEM((2, 3, TOK, HD), bf16),
            pltpu.VMEM((3 * TOK, wide), f32),
            pltpu.VMEM((TOK, wide), bf16),
            pltpu.VMEM((3 * TOK, wide), bf16),
            pltpu.VMEM((3 * TOK, wide), bf16),
            pltpu.VMEM((8, TOK), f32),
            pltpu.VMEM((TOK, TOK), f32),
            pltpu.VMEM((2, 3, TOK, HD), f32),
            pltpu.VMEM((HD, wide), f32),
            pltpu.VMEM((TOK, GROUP * HD), bf16),
            pltpu.VMEM((2, TOK, HD), bf16),
            pltpu.VMEM((2, 2, TOK, HD), bf16),
            pltpu.VMEM((2, 2, TOK, HD), bf16),
            pltpu.VMEM((32, 1, 128), f32),
            pltpu.VMEM((16, 1, 128), f32),
            pltpu.VMEM((2, 1, 128), f32),
            dma((6,)),
            dma((3,)),
            dma((2, 3)),
            dma((2, 3)),
            dma((2, 2)),
            dma((2, 2)),
            dma((2, 31)),
            dma((2, 31)),
        ],
        compiler_params=pltpu.CompilerParams(
            collective_id=0, has_side_effects=True, vmem_limit_bytes=56 * 2**20
        ),
        name="grads",
    )(queries, keys, values, out_grad, outputs, block_ids)
    gq, gk, gv = pl.pallas_call(
        place_outputs,
        out_shape=tuple(jax.ShapeDtypeStruct(x.shape, x.dtype) for x in (gq, gk, gv)),
        in_specs=[hbm] * 3,
        out_specs=(hbm,) * 3,
        scratch_shapes=[
            pltpu.VMEM((TOK, GROUP * HD), bf16),
            pltpu.VMEM((2, TOK, HD), bf16),
            dma((6,)),
            dma((6,)),
        ],
        name="place_outputs",
    )(gq, gk, gv)
    return gq, gk, gv, square.reshape(())


def solution(mesh):
    return jax.shard_map(
        shards,
        mesh=mesh,
        in_specs=(
            P("ctx", "head"),
            P("ctx", "head"),
            P("ctx", "head"),
            P("ctx", "head"),
            P("ctx", "head"),
            P(),
        ),
        out_specs=(P("ctx", "head"), P("ctx", "head"), P("ctx", "head"), P()),
        check_vma=False,
    )
```
